512 devices in a mesh: replica: 32 (over x_lo, y, core), tensor: 16 (over z, x_hi).
Axes of the slice: x: 4 (x_hi: 2, x_lo: 2; x = x_hi * 2 + x_lo), y: 8, z: 8, core: 2. Of those that a mesh axis runs over, the one named last changes fastest.
Arguments:
- hidden: bfloat16 [2, 1, 16384, 12288], P(None, None, 'replica', 'tensor'), may hold values from -6 to 6
- queries: bfloat16 [2, 1, 16384, 6144], P(None, None, ('replica', 'tensor')), may hold values from -160 to 160
- kv_cache: bfloat16 [1, 16384, 16, 1024], P(None, ('replica', 'tensor')), may hold values from -6 to 6
- lengths: int32 [16384], P(('replica', 'tensor')), may hold values from 2 to 16, as said below
- versions: int32 [32, 1], replicated, may hold values from 0 to 1, as said below
- resident: bfloat16 [1, 12288, 1024], P(None, 'tensor'), may hold values from -0.0546875 to 0.0546875
- update: bfloat16 [1, 12288, 1024], P(None, ('tensor', 'replica')), may hold values from -0.0546875 to 0.0546875
Outputs:
- attended: bfloat16 [2, 1, 16384, 6144], P(None, None, ('replica', 'tensor'))
The draws below stay inside these ranges and needn't reach their ends.
Inputs may be any that keep to these rules, and one draw needn't show every extreme that they name: `lengths`: some row has exactly 16. `versions`: in every layer some replica runs version 1 and some runs version 0.
All inputs are finite; a program needn't handle non-finite values.
Results may differ from the reference program's by a relative error of at most 0.0054.
Values may be sent and summed in bfloat16 or wider, within the bound.
No kernel may reach another device: no remote copies, remote signals or barrier semaphores. Data moves between devices by JAX's collectives and lax.ppermute only.
A program may use at most 64 MiB of HBM per device.

```python
import math
import jax
import jax.numpy as jnp
from jax import lax

D = 12288
HEAD = 128
QPK = 12
KVH = 4
LAYERS = 1
STEPS = 2
ROWS = 512
POS = 16
KVW = 1024
ALLROWS = 16384
N_REPLICA = 32


def draw_kv_cache(key, part):
    key = jax.random.fold_in(key, 11)
    full_shape = (LAYERS, ALLROWS, POS, KVW)
    return jax.random.truncated_normal(key, -6.0, 6.0, full_shape, jnp.float32).astype(jnp.bfloat16)


def draw_queries(key, part):
    key = jax.random.fold_in(key, 12)
    full_shape = (STEPS, LAYERS, ALLROWS, KVH * QPK * HEAD)
    return jax.random.truncated_normal(key, -6.0, 6.0, full_shape, jnp.float32).astype(jnp.bfloat16)


def draw_lengths(key, part):
    key = jax.random.fold_in(key, 13)
    values = jax.random.randint(key, (ALLROWS,), 2, POS + 1, dtype=jnp.int32)
    chosen = jax.random.randint(jax.random.fold_in(key, 1), (), 0, ALLROWS, dtype=jnp.int32)
    return jnp.where(jnp.arange(ALLROWS, dtype=jnp.int32) == chosen, POS, values).astype(jnp.int32)


def draw_versions(key, part):
    key = jax.random.fold_in(key, 14)
    values = jax.random.randint(key, (N_REPLICA, LAYERS), 0, 2, dtype=jnp.int32)
    first_pick = jax.random.randint(jax.random.fold_in(key, 1), (LAYERS,), 0, N_REPLICA, dtype=jnp.int32)
    step_pick = jax.random.randint(jax.random.fold_in(key, 2), (LAYERS,), 1, N_REPLICA, dtype=jnp.int32)
    second_pick = (first_pick + step_pick) % N_REPLICA
    replica_ids = jnp.arange(N_REPLICA, dtype=jnp.int32)[:, None]
    values = jnp.where(replica_ids == first_pick[None, :], 1, values)
    values = jnp.where(replica_ids == second_pick[None, :], 0, values)
    return values.astype(jnp.int32)


def block_levels(rng, extent, shards, least, high):
    level = 1.0
    for axis_at, parts in shards:
        steps = jax.random.uniform(jax.random.fold_in(jax.random.fold_in(rng, 6), axis_at), (parts,), jnp.float32, least / len(shards), high / len(shards))
        level = level * jnp.repeat(jnp.exp(steps), extent[axis_at] // parts).reshape((-1,) + (1,) * (len(extent) - 1 - axis_at))
    return level


def gaussian(key, dims, scale, most, pieces=(), kind=jnp.bfloat16):
    loudness = block_levels(key, dims, pieces, -0.22, 0.18) if pieces else 1.0
    entries = jax.random.normal(key, dims, jnp.float32) * scale * loudness
    return jnp.minimum(jnp.maximum(entries, -most), most).astype(kind)


def setup_inputs(seed: int = 0) -> dict:
    keys = jax.random.split(jax.random.key(seed), 8)
    hidden = gaussian(keys[0], (STEPS, LAYERS, ALLROWS, D), 1.0, 6.0, ((2, 32), (3, 16)))
    queries = draw_queries(jax.random.fold_in(keys[7], 71), 0)
    kv_cache = draw_kv_cache(jax.random.fold_in(keys[7], 71), 0)
    lengths = draw_lengths(jax.random.fold_in(keys[7], 71), 0)
    versions = draw_versions(jax.random.fold_in(keys[7], 71), 0)
    resident = gaussian(keys[5], (LAYERS, D, KVW), D ** -0.5, 0.0546875, ((1, 16),))
    update = gaussian(keys[6], (LAYERS, D, KVW), D ** -0.5, 0.0546875, ((1, 512),))
    return {"hidden": hidden, "queries": queries, "kv_cache": kv_cache, "lengths": lengths, "versions": versions, "resident": resident, "update": update}


THETA = 1000000.0

def rounded(value):
    return lax.optimization_barrier(value.astype(jnp.bfloat16)).astype(jnp.float32)

def rotate_keys(kv_sum, positions):
    lead_shape = kv_sum.shape[:-1]
    key_width = KVH * HEAD
    key_part = kv_sum[..., :key_width].reshape(lead_shape + (KVH, HEAD))
    half_head = HEAD // 2
    inverse = THETA ** (-(jnp.arange(half_head, dtype=jnp.float32) * 2.0 / HEAD))
    angles = positions[..., None, None] * inverse
    cosine_table = jnp.cos(angles)
    sine_table = jnp.sin(angles)
    front_half = key_part[..., :half_head]
    back_half = key_part[..., half_head:]
    rotated = jnp.concatenate([front_half * cosine_table - back_half * sine_table, back_half * cosine_table + front_half * sine_table], -1)
    return jnp.concatenate([rotated.reshape(lead_shape + (key_width,)), kv_sum[..., key_width:]], -1)

def attend(query_rows, cache_rows, kv_new, lengths):
    step_count = query_rows.shape[0]
    row_count = query_rows.shape[1]
    slot_count = cache_rows.shape[1]
    key_width = KVH * HEAD
    highest_precision = lax.Precision.HIGHEST
    query_heads = query_rows.reshape(step_count, row_count, KVH, QPK, HEAD).astype(jnp.float32)
    cache_keys = cache_rows[:, :, :key_width].reshape(row_count, slot_count, KVH, HEAD).astype(jnp.float32)
    cache_values = cache_rows[:, :, key_width:].reshape(row_count, slot_count, KVH, HEAD).astype(jnp.float32)
    new_keys = kv_new[..., :key_width].reshape(step_count, row_count, KVH, HEAD).astype(jnp.float32)
    new_values = kv_new[..., key_width:].reshape(step_count, row_count, KVH, HEAD).astype(jnp.float32)
    score_scale = 1.0 / math.sqrt(HEAD)
    cache_scores = jnp.einsum('srgjd,rpgd->srgjp', query_heads, cache_keys, precision=highest_precision) * score_scale
    new_scores = jnp.einsum('srgjd,trgd->srgjt', query_heads, new_keys, precision=highest_precision) * score_scale
    filled = jnp.arange(slot_count, dtype=jnp.int32)[None, :] < lengths[:, None]
    cache_scores = jnp.where(filled[None, :, None, None, :], cache_scores, -1e+30)
    causal = jnp.arange(step_count, dtype=jnp.int32)[None, :] <= jnp.arange(step_count, dtype=jnp.int32)[:, None]
    new_scores = jnp.where(causal[:, None, None, None, :], new_scores, -1e+30)
    highest = jnp.maximum(lax.optimization_barrier(jnp.max(cache_scores, -1)), lax.optimization_barrier(jnp.max(new_scores, -1)))[..., None]
    cache_exp = jnp.exp(cache_scores - highest)
    new_exp = jnp.exp(new_scores - highest)
    denominator = lax.optimization_barrier(jnp.sum(cache_exp, -1, keepdims=True)) + lax.optimization_barrier(jnp.sum(new_exp, -1, keepdims=True))
    cache_weights = rounded(cache_exp / denominator)
    new_weights = rounded(new_exp / denominator)
    attended = jnp.einsum('srgjp,rpgd->srgjd', cache_weights, cache_values, precision=highest_precision)
    attended = attended + jnp.einsum('srgjt,trgd->srgjd', new_weights, new_values, precision=highest_precision)
    return attended.reshape(step_count, row_count, KVH * QPK * HEAD).astype(jnp.bfloat16)

def reference(hidden, queries, kv_cache, lengths, versions, resident, update):
    results = []
    for layer_index in range(LAYERS):
        old_weight = resident[layer_index]
        new_weight = update[layer_index]

        def project(operands):
            replica_rows, version = operands
            weight = jnp.where(version == 1, new_weight, old_weight).astype(jnp.float32)
            return jnp.einsum('srd,dk->srk', replica_rows.astype(jnp.float32), weight, precision=lax.Precision.HIGHEST)
        grouped = hidden[:, layer_index].reshape(STEPS, N_REPLICA, ROWS, D).transpose(1, 0, 2, 3)
        summed = lax.map(project, (grouped, versions[:, layer_index]))
        summed = summed.transpose(1, 0, 2, 3).reshape(STEPS, ALLROWS, KVW)
        positions = (lengths[None, :] + jnp.arange(STEPS, dtype=jnp.int32)[:, None]).astype(jnp.float32)
        kv_new = rounded(rotate_keys(summed, positions))
        results.append(attend(queries[:, layer_index], kv_cache[layer_index], kv_new, lengths))
    return jnp.stack(results, 1)
```

```python
import functools
import math

import jax
import jax.numpy as jnp
from jax import lax
from jax.experimental import pallas as pl
from jax.experimental.pallas import tpu as pltpu
from jax.sharding import PartitionSpec as P

HEAD = 128
QPK = 12
KVH = 4
BLOCK = 16
MASKED = -1e30

def _queries(q_ref, steps, rows, start):
    return jnp.concatenate(
        [q_ref[s*rows+start:s*rows+start+BLOCK, j*HEAD:(j+1)*HEAD] for j in range(QPK) for s in range(steps)], 0)

def _scores(q, k):
    return lax.dot_general(q, k, (((1,), (1,)), ((), ())), preferred_element_type=jnp.float32) * (1.0/math.sqrt(HEAD))

def cache_kernel(q_ref, keys_ref, values_ref, bias_ref, acc_ref, stat_ref, *, steps, rows, slots):
    span = BLOCK*slots
    for half in range(rows//BLOCK):
        q = _queries(q_ref, steps, rows, half*BLOCK)
        n = q.shape[0]
        keys = keys_ref[half*span:(half+1)*span, :]
        values = values_ref[half*span:(half+1)*span, :]
        s = _scores(q, keys).reshape(n//BLOCK, BLOCK, span) + bias_ref[half*BLOCK:(half+1)*BLOCK, :][None]
        s = s.reshape(n, span)
        peak = jnp.max(s, -1, keepdims=True)
        p = jnp.exp(s - peak)
        total = jnp.sum(p, -1, keepdims=True)
        acc_ref[0, half*n:(half+1)*n, :] = jnp.dot(p.astype(jnp.bfloat16), values, preferred_element_type=jnp.float32)
        lane = lax.broadcasted_iota(jnp.int32, (n, HEAD), 1)
        stat_ref[0, half*n:(half+1)*n, :] = jnp.where(lane < HEAD//2, peak, total)

def finish_kernel(q_ref, ksum_ref, vsum_ref, cos_ref, sin_ref, bias_ref, acc_ref, stat_ref, out_ref, *, steps, rows):
    k = jnp.sum(ksum_ref[...].astype(jnp.float32), 0)
    k = (k*cos_ref[...] + pltpu.roll(k, HEAD//2, 1)*sin_ref[...]).astype(jnp.bfloat16)
    v = jnp.sum(vsum_ref[...].astype(jnp.float32), 0).astype(jnp.bfloat16)
    for half in range(rows//BLOCK):
        q = _queries(q_ref, steps, rows, half*BLOCK)
        n = q.shape[0]
        pick = lambda x: jnp.concatenate([x[t*rows+half*BLOCK:t*rows+(half+1)*BLOCK] for t in range(steps)], 0)
        s = _scores(q, pick(k)).reshape(QPK, steps*BLOCK, steps*BLOCK) + bias_ref[...][None]
        s = s.reshape(n, steps*BLOCK)
        stat = stat_ref[0, half*n:(half+1)*n, :]
        old_peak = stat[:, :1]; old_total = stat[:, HEAD//2:HEAD//2+1]
        peak = jnp.maximum(old_peak, jnp.max(s, -1, keepdims=True))
        p = jnp.exp(s - peak)
        keep = jnp.exp(old_peak - peak)
        inv = 1.0 / (old_total*keep + jnp.sum(p, -1, keepdims=True))
        out = acc_ref[0, half*n:(half+1)*n, :]*(keep*inv) + jnp.dot((p*inv).astype(jnp.bfloat16), pick(v), preferred_element_type=jnp.float32)
        out = out.astype(out_ref.dtype)
        for j in range(QPK):
            for t in range(steps):
                at = (j*steps+t)*BLOCK
                out_ref[t*rows+half*BLOCK:t*rows+(half+1)*BLOCK, j*HEAD:(j+1)*HEAD] = out[at:at+BLOCK]

def cache_part(q, kv, lengths):
    steps, rows, width = q.shape
    slots = kv.shape[1]
    wide = QPK*HEAD
    col = jnp.arange(BLOCK*slots, dtype=jnp.int32)[None]
    row = jnp.arange(rows, dtype=jnp.int32)[:, None]
    bias = jnp.where((col//slots == row % BLOCK) & (col % slots < lengths[:, None]), 0.0, MASKED).astype(jnp.float32)
    tall = QPK*steps*rows
    return pl.pallas_call(
        functools.partial(cache_kernel, steps=steps, rows=rows, slots=slots),
        grid=(KVH,),
        in_specs=[pl.BlockSpec((steps*rows, wide), lambda g: (0, g)),
                  pl.BlockSpec((rows*slots, HEAD), lambda g: (0, g)),
                  pl.BlockSpec((rows*slots, HEAD), lambda g: (0, KVH+g)),
                  pl.BlockSpec((rows, BLOCK*slots), lambda g: (0, 0))],
        out_specs=[pl.BlockSpec((1, tall, HEAD), lambda g: (g, 0, 0))]*2,
        out_shape=[jax.ShapeDtypeStruct((KVH, tall, HEAD), jnp.float32)]*2,
        cost_estimate=pl.CostEstimate(flops=4*KVH*tall*BLOCK*slots*HEAD, bytes_accessed=6<<20, transcendentals=KVH*tall*BLOCK*slots),
        compiler_params=pltpu.CompilerParams(vmem_limit_bytes=32<<20),
        name="cache_part",
    )(q.reshape(steps*rows, width), kv.reshape(rows*slots, 2*KVH*HEAD), kv.reshape(rows*slots, 2*KVH*HEAD), bias)

THETA=1000000.0
def tables(lengths, steps):
    positions = (lengths[None, :] + jnp.arange(steps, dtype=jnp.int32)[:, None]).astype(jnp.float32)
    inverse = THETA ** (-(jnp.arange(HEAD//2, dtype=jnp.float32) * 2.0 / HEAD))
    angles = (positions[..., None]*inverse).reshape(-1, HEAD//2)
    c, s = jnp.cos(angles), jnp.sin(angles)
    return jnp.concatenate([c, c], -1), jnp.concatenate([-s, s], -1)

def finish(q, kv_sum, cos, sin, acc, stat):
    steps, rows, width = q.shape
    wide = QPK*HEAD
    tall = acc.shape[1]
    at = jnp.arange(steps*BLOCK, dtype=jnp.int32)
    ok = (at[:, None] % BLOCK == at[None] % BLOCK) & (at[None]//BLOCK <= at[:, None]//BLOCK)
    bias = jnp.where(ok, 0.0, MASKED).astype(jnp.float32)
    n = steps*rows
    pieces = kv_sum.shape[0]
    out = pl.pallas_call(
        functools.partial(finish_kernel, steps=steps, rows=rows),
        grid=(KVH,),
        in_specs=[pl.BlockSpec((n, wide), lambda g: (0, g)),
                  pl.BlockSpec((pieces, n, HEAD), lambda g: (0, 0, g)),
                  pl.BlockSpec((pieces, n, HEAD), lambda g: (0, 0, KVH+g)),
                  pl.BlockSpec((n, HEAD), lambda g: (0, 0)),
                  pl.BlockSpec((n, HEAD), lambda g: (0, 0)),
                  pl.BlockSpec((steps*BLOCK, steps*BLOCK), lambda g: (0, 0)),
                  pl.BlockSpec((1, tall, HEAD), lambda g: (g, 0, 0)),
                  pl.BlockSpec((1, tall, HEAD), lambda g: (g, 0, 0))],
        out_specs=pl.BlockSpec((n, wide), lambda g: (0, g)),
        out_shape=jax.ShapeDtypeStruct((n, width), jnp.bfloat16),
        compiler_params=pltpu.CompilerParams(vmem_limit_bytes=32<<20),
        name="finish",
    )(q.reshape(n, width), kv_sum, kv_sum, cos, sin, bias, acc, stat)
    return out.reshape(steps, rows, width)


def per_device(hidden, queries, kv_cache, lengths, versions, resident, update):
    steps, _, rows, width = hidden.shape
    replicas, shards = lax.axis_size("replica"), lax.axis_size("tensor")
    local = rows // shards
    x = hidden[:, 0].reshape(steps, shards, local, width).transpose(1, 0, 2, 3).reshape(rows*steps, width)
    cores = [[r for r in range(replicas) if r % 2 == c] for c in range(2)]
    mine = lax.all_gather(update[0], "replica", axis=0, axis_index_groups=cores)
    other = lax.ppermute(mine, "replica", [(r, r ^ 1) for r in range(replicas)])
    odd = lax.axis_index("replica") % 2 == 1
    new = jnp.where(odd, jnp.stack([other, mine], 1), jnp.stack([mine, other], 1)).reshape(resident.shape[1:])
    version = lax.dynamic_index_in_dim(versions[:, 0], lax.axis_index("replica"), 0, keepdims=False)
    chosen = jnp.where(version == 1, new, resident[0])
    partial = jnp.dot(x, chosen, preferred_element_type=jnp.float32).astype(jnp.bfloat16)
    pieces = lax.all_to_all(partial.reshape(shards, steps*local, -1), "tensor", 0, 0, tiled=True)
    acc, stat = cache_part(queries[:, 0], kv_cache[0], lengths)
    cos, sin = tables(lengths, steps)
    return finish(queries[:, 0], pieces, cos, sin, acc, stat)[:, None]


def solution(mesh):
    placed = (
        P(None, None, "replica", "tensor"),
        P(None, None, ("replica", "tensor"), None),
        P(None, ("replica", "tensor"), None, None),
        P(("replica", "tensor")),
        P(),
        P(None, "tensor", None),
        P(None, ("tensor", "replica"), None),
    )
    return jax.shard_map(
        per_device,
        mesh=mesh,
        in_specs=placed,
        out_specs=P(None, None, ("replica", "tensor"), None),
        check_vma=False,
    )
```

```python
import functools
import math

import jax
import jax.numpy as jnp
from jax import lax
from jax.experimental import pallas as pl
from jax.experimental.pallas import tpu as pltpu
from jax.sharding import PartitionSpec as P

HEAD = 128
QPK = 12
KVH = 4
BLOCK = 16
MASKED = -1e30
SCALE = 1.0 / math.sqrt(HEAD)
THETA = 1000000.0
WIDE = QPK * HEAD
YS = 8
ANY = pl.BlockSpec(memory_space=pl.ANY)
VM = pl.BlockSpec(memory_space=pltpu.VMEM)
SM = pl.BlockSpec(memory_space=pltpu.SMEM)
GRANT = 24 << 20

def _queries(q_ref, steps, rows, start, g):
    return jnp.concatenate(
        [q_ref[s*rows+start:s*rows+start+BLOCK, g*WIDE+j*HEAD:g*WIDE+(j+1)*HEAD] for j in range(QPK) for s in range(steps)], 0)

def cache_kernel(q_ref, kv_ref, bias_ref, acc_ref, stat_ref, *, steps, rows, slots):
    span = BLOCK*slots
    n = QPK*steps*BLOCK
    lane = lax.broadcasted_iota(jnp.int32, (n, HEAD), 1)
    stat = jnp.zeros((n, HEAD), jnp.float32)
    for half in range(rows//BLOCK):
        at = slice(half*n, (half+1)*n)
        bias = bias_ref[half*BLOCK:(half+1)*BLOCK, :]
        for g in range(KVH):
            q = _queries(q_ref, steps, rows, half*BLOCK, g)
            keys = kv_ref[half*span:(half+1)*span, g*HEAD:(g+1)*HEAD]
            values = kv_ref[half*span:(half+1)*span, (KVH+g)*HEAD:(KVH+g+1)*HEAD]
            s = lax.dot_general(q, keys, (((1,), (1,)), ((), ())), preferred_element_type=jnp.float32) * SCALE
            s = (s.reshape(n//BLOCK, BLOCK, span) + bias[None]).reshape(n, span)
            peak = jnp.max(s, -1, keepdims=True)
            p = jnp.exp(s - peak).astype(jnp.bfloat16)
            both = jnp.dot(p, jnp.concatenate([values, jnp.ones_like(values)], 1), preferred_element_type=jnp.float32)
            acc_ref[g, at, :] = both[:, :HEAD]
            spot = 2*(half*KVH+g)
            stat = jnp.where(lane == spot, peak, jnp.where(lane == spot+1, both[:, HEAD:], stat))
    stat_ref[...] = stat

def finish_kernel(q_ref, sum_ref, cos_ref, sin_ref, bias_ref, acc_ref, stat_ref, out_ref, held, sems, *, steps, rows):
    copies = []
    pieces = sum_ref.shape[0]
    n = QPK*steps*BLOCK
    for g in range(KVH):
        cols = slice(g*HEAD, (g+1)*HEAD)
        k = sum_ref[0, 0, :, cols].astype(jnp.float32)
        v = sum_ref[0, 1, :, cols].astype(jnp.float32)
        for i in range(1, pieces):
            k = k + sum_ref[i, 0, :, cols].astype(jnp.float32)
            v = v + sum_ref[i, 1, :, cols].astype(jnp.float32)
        k = (k*cos_ref[...] + pltpu.roll(k, HEAD//2, 1)*sin_ref[...]).astype(jnp.bfloat16)
        v = v.astype(jnp.bfloat16)
        v = jnp.concatenate([v, jnp.ones_like(v)], 1)
        for half in range(rows//BLOCK):
            q = _queries(q_ref, steps, rows, half*BLOCK, g)
            pick = lambda x: jnp.concatenate([x[t*rows+half*BLOCK:t*rows+(half+1)*BLOCK] for t in range(steps)], 0)
            s = lax.dot_general(q, pick(k), (((1,), (1,)), ((), ())), preferred_element_type=jnp.float32) * SCALE
            s = (s.reshape(QPK, steps*BLOCK, steps*BLOCK) + bias_ref[...][None]).reshape(n, steps*BLOCK)
            at = slice(half*n, (half+1)*n)
            spot = 2*(half*KVH+g)
            old = jnp.broadcast_to(stat_ref[:, spot:spot+1], (n, HEAD))
            total = jnp.broadcast_to(stat_ref[:, spot+1:spot+2], (n, HEAD))
            peak = jnp.maximum(old, jnp.max(s, -1, keepdims=True))
            p = jnp.exp(s - peak[:, :steps*BLOCK]).astype(jnp.bfloat16)
            both = jnp.dot(p, pick(v), preferred_element_type=jnp.float32)
            keep = jnp.exp(old - peak)
            out = (acc_ref[g, at, :]*keep + both[:, :HEAD]) / (total*keep + both[:, HEAD:])
            out = out.astype(held.dtype)
            for j in range(QPK):
                for t in range(steps):
                    b = (j*steps+t)*BLOCK
                    held[t*rows+half*BLOCK:t*rows+(half+1)*BLOCK, g*WIDE+j*HEAD:g*WIDE+(j+1)*HEAD] = out[b:b+BLOCK]
        part = slice(g*WIDE, (g+1)*WIDE)
        copies.append(pltpu.make_async_copy(held.at[:, part], out_ref.at[:, part], sems.at[g]))
        copies[-1].start()
    for copy in copies:
        copy.wait()

def cache_part(q, kv, lengths):
    steps, rows, width = q.shape
    slots = kv.shape[1]
    col = jnp.arange(BLOCK*slots, dtype=jnp.int32)[None]
    row = jnp.arange(rows, dtype=jnp.int32)[:, None]
    bias = jnp.where((col//slots == row % BLOCK) & (col % slots < lengths[:, None]), 0.0, MASKED).astype(jnp.float32)
    tall = QPK*steps*rows
    return pl.pallas_call(
        functools.partial(cache_kernel, steps=steps, rows=rows, slots=slots),
        in_specs=[VM]*3, out_specs=[VM]*2,
        out_shape=[jax.ShapeDtypeStruct((KVH, tall, HEAD), jnp.float32), jax.ShapeDtypeStruct((QPK*steps*BLOCK, HEAD), jnp.float32)],
        cost_estimate=pl.CostEstimate(flops=4*KVH*tall*BLOCK*slots*HEAD, bytes_accessed=6<<20, transcendentals=KVH*tall*BLOCK*slots),
        compiler_params=pltpu.CompilerParams(vmem_limit_bytes=GRANT),
        name="cache_part",
    )(q.reshape(steps*rows, width), kv.reshape(rows*slots, 2*KVH*HEAD), bias)

def tables(lengths, steps):
    positions = (lengths[None, :] + jnp.arange(steps, dtype=jnp.int32)[:, None]).astype(jnp.float32)
    inverse = THETA ** (-(jnp.arange(HEAD//2, dtype=jnp.float32) * 2.0 / HEAD))
    angles = (positions[..., None]*inverse).reshape(-1, HEAD//2)
    c, s = jnp.cos(angles), jnp.sin(angles)
    return jnp.concatenate([c, c], -1), jnp.concatenate([-s, s], -1)

def finish(q, kv_sum, cos, sin, stats):
    steps, rows, width = q.shape
    at = jnp.arange(steps*BLOCK, dtype=jnp.int32)
    ok = (at[:, None] % BLOCK == at[None] % BLOCK) & (at[None]//BLOCK <= at[:, None]//BLOCK)
    bias = jnp.where(ok, 0.0, MASKED).astype(jnp.float32)
    n = steps*rows
    pieces = kv_sum.shape[0]//2
    out = pl.pallas_call(
        functools.partial(finish_kernel, steps=steps, rows=rows),
        in_specs=[VM]*7, out_specs=ANY,
        scratch_shapes=[pltpu.VMEM((n, width), jnp.bfloat16), pltpu.SemaphoreType.DMA((KVH,))],
        out_shape=jax.ShapeDtypeStruct((n, width), jnp.bfloat16),
        compiler_params=pltpu.CompilerParams(vmem_limit_bytes=GRANT),
        name="finish",
    )(q.reshape(n, width), kv_sum.reshape(pieces, 2, n, KVH*HEAD), cos, sin, bias, *stats)
    return out.reshape(steps, rows, width)

CHUNK = 256


def pieces_kernel(update_ref, out_ref):
    wide = out_ref.shape[2]
    for i in range(out_ref.shape[0]):
        at = (i // 4) * 2 + i % 2
        out_ref[i] = update_ref[:, at * wide : (at + 1) * wide]


def outgoing_kernel(served_ref, x_ref, resident_ref, out_ref, x_held, weight, versions_ref, sems, *, first):
    rows, depth = out_ref.shape
    wide = weight.shape[1]
    chunks = [slice(i, i + CHUNK) for i in range(0, rows, CHUNK)]
    count = len(chunks)
    cols = pl.ds(pl.multiple_of((1 - lax.axis_index("tensor") % 2) * wide, wide), wide)
    load = pltpu.make_async_copy(resident_ref.at[:, cols], weight, sems.at[2 * count])
    arrivals = [pltpu.make_async_copy(x_ref.at[first + c.start : first + c.stop], x_held.at[c], sems.at[n]) for n, c in enumerate(chunks)]
    leaving = [pltpu.make_async_copy(x_held.at[c], out_ref.at[c], sems.at[count + n]) for n, c in enumerate(chunks)]
    short = [pltpu.make_async_copy(x_held.at[c, :wide], out_ref.at[c, :wide], sems.at[count + n]) for n, c in enumerate(chunks)]

    which = pltpu.make_async_copy(served_ref, versions_ref, sems.at[2 * count + 1])
    which.start()
    arrivals[0].start()
    load.start()
    for copy in arrivals[1:]:
        copy.start()
    which.wait()
    fresh = versions_ref[lax.axis_index("replica")] == 1

    @pl.when(fresh)
    def _():
        for n in range(count):
            arrivals[n].wait()
            leaving[n].start()
        load.wait()
        for copy in leaving:
            copy.wait()

    @pl.when(jnp.logical_not(fresh))
    def _():
        load.wait()
        for n, c in enumerate(chunks):
            arrivals[n].wait()
            part = jnp.dot(x_held[c], weight[...], preferred_element_type=jnp.float32)
            x_held[c, :wide] = part.astype(x_held.dtype)
            short[n].start()
        for copy in short:
            copy.wait()


def outgoing(served, x, resident, first, rows):
    depth, wide = x.shape[1], resident.shape[1] // 2
    return pl.pallas_call(
        functools.partial(outgoing_kernel, first=first),
        in_specs=[ANY] * 3,
        out_specs=ANY,
        out_shape=jax.ShapeDtypeStruct((rows, depth), x.dtype),
        scratch_shapes=[
            pltpu.VMEM((rows, depth), x.dtype),
            pltpu.VMEM((depth, wide), x.dtype),
            pltpu.SMEM(served.shape, jnp.int32),
            pltpu.SemaphoreType.DMA((2 * (rows // CHUNK) + 2,)),
        ],
        compiler_params=pltpu.CompilerParams(vmem_limit_bytes=60 << 20),
        name="outgoing",
    )(served, x, resident)


def project_kernel(versions_ref, own_ref, pair_ref, resident_ref, mine_ref, other_ref, out_ref, weight_ref, held, sems):
    depth, wide = own_ref.shape[-1], resident_ref.shape[1] // 2
    steps, shards = own_ref.shape[:2]
    ycount, tall, quarter = mine_ref.shape
    chunk = tall // 4
    high, core = lax.axis_index("tensor") % 2, lax.axis_index("replica") % 2
    fresh = versions_ref[lax.axis_index("replica")] == 1
    blocks = CHUNK // (steps * own_ref.shape[2])

    def rows(ref, i, cols):
        return jnp.concatenate([ref[s, i + b, :, cols] for b in range(blocks) for s in range(steps)], 0)

    def send(i, out):
        held[i : i + blocks] = out.astype(held.dtype).reshape(blocks, -1, wide)
        pltpu.make_async_copy(held.at[i : i + blocks], out_ref.at[i : i + blocks], sems.at[i // blocks]).start()

    @pl.when(fresh)
    def _():
        for got, at in ((mine_ref, core), (other_ref, 1 - core)):
            cols = pl.ds(pl.multiple_of(at * quarter, quarter), quarter)
            for block, source in ((0, high), (1, 1 - high)):
                for low in range(2):
                    take = pl.ds(pl.multiple_of((source * 2 + low) * chunk, chunk), chunk)
                    for y in range(ycount):
                        to = block * depth + (low * ycount + y) * chunk
                        weight_ref[to : to + chunk, cols] = got[y, take, :]
        for i in range(0, shards, blocks):
            out = jnp.dot(rows(own_ref, i, slice(None)), weight_ref[:depth, :], preferred_element_type=jnp.float32)
            send(i, out + jnp.dot(rows(pair_ref, i, slice(None)), weight_ref[depth:, :], preferred_element_type=jnp.float32))

    @pl.when(jnp.logical_not(fresh))
    def _():
        cols = pl.ds(pl.multiple_of(high * wide, wide), wide)
        for i in range(0, shards, blocks):
            out = jnp.dot(rows(own_ref, i, slice(None)), resident_ref[:, cols], preferred_element_type=jnp.float32)
            send(i, out + rows(pair_ref, i, slice(0, wide)).astype(jnp.float32))

    for i in range(0, shards, blocks):
        pltpu.make_async_copy(held.at[i : i + blocks], out_ref.at[i : i + blocks], sems.at[i // blocks]).wait()


def call(kernel, specs, out_specs, out_shape, scratch=(), name=None):
    return pl.pallas_call(
        kernel,
        in_specs=specs,
        out_specs=out_specs,
        out_shape=out_shape,
        scratch_shapes=scratch,
        compiler_params=pltpu.CompilerParams(vmem_limit_bytes=GRANT),
        name=name,
    )


def per_device(hidden, queries, kv_cache, lengths, versions, resident, update):
    steps, _, rows, width = hidden.shape
    replicas, shards = lax.axis_size("replica"), lax.axis_size("tensor")
    both = ("replica", "tensor")
    kind = hidden.dtype
    piece, wide = update.shape[1], update.shape[2] // 2
    served = versions[:, 0]
    groups = [
        [((a * YS + b) * 2 + c) * shards + z * 2 + h for h in range(2) for a in range(2) for c in range(2)]
        for b in range(YS)
        for z in range(shards // 2)
    ]
    lines = [[(a * YS + b) * 2 + c for b in range(YS)] for a in range(2) for c in range(2)]
    pieces = call(pieces_kernel, [pl.BlockSpec()], pl.BlockSpec(), jax.ShapeDtypeStruct((8, piece, wide // 2), kind), name="pieces")(pltpu.with_memory_space_constraint(update[0], pltpu.HBM))
    got = lax.all_to_all(pieces, both, 0, 0, axis_index_groups=groups, tiled=True)
    message = outgoing(served, hidden.reshape(steps * rows, width), resident[0], 0, steps * rows)
    got, message = lax.optimization_barrier((got, message))
    pair = lax.ppermute(message, "tensor", [(i, i ^ 1) for i in range(shards)])
    mine = lax.all_gather(got.reshape(-1, wide // 2), "replica", axis=0, axis_index_groups=lines)
    other = lax.ppermute(mine, "replica", [(i, i ^ 1) for i in range(replicas)])
    local = rows // shards
    partial = pltpu.HBM((shards, steps * local, wide), kind)
    scratch = [pltpu.VMEM((2 * width, wide), kind), pltpu.VMEM(partial.shape, kind), pltpu.SemaphoreType.DMA((steps * rows // CHUNK,))]
    partial = call(project_kernel, [SM] + [VM] * 5, ANY, partial, scratch, "project")(
        served, hidden.reshape(steps, shards, local, width), pair.reshape(steps, shards, local, width), resident[0], mine, other
    )
    summands = lax.all_to_all(partial, "tensor", 0, 0, tiled=True)
    stats = cache_part(queries[:, 0], kv_cache[0], lengths)
    cos, sin = tables(lengths, steps)
    return finish(queries[:, 0], summands, cos, sin, stats)[:, None]


def solution(mesh):
    placed = (
        P(None, None, "replica", "tensor"),
        P(None, None, ("replica", "tensor"), None),
        P(None, ("replica", "tensor"), None, None),
        P(("replica", "tensor")),
        P(),
        P(None, "tensor", None),
        P(None, ("tensor", "replica"), None),
    )
    return jax.shard_map(
        per_device,
        mesh=mesh,
        in_specs=placed,
        out_specs=P(None, None, ("replica", "tensor"), None),
        check_vma=False,
    )
```

```python
import functools
import math

import jax
import jax.numpy as jnp
from jax import lax
from jax.experimental import pallas as pl
from jax.experimental.pallas import tpu as pltpu
from jax.sharding import PartitionSpec as P

HEAD = 128
QPK = 12
KVH = 4
BLOCK = 16
MASKED = -1e30
SCALE = 1.0 / math.sqrt(HEAD)
THETA = 1000000.0
WIDE = QPK * HEAD
YS = 8
ANY = pl.BlockSpec(memory_space=pl.ANY)
VM = pl.BlockSpec(memory_space=pltpu.VMEM)
SM = pl.BlockSpec(memory_space=pltpu.SMEM)
GRANT = 24 << 20

def _queries(q_ref, steps, rows, start, g):
    return jnp.concatenate(
        [q_ref[s*rows+start:s*rows+start+BLOCK, g*WIDE+j*HEAD:g*WIDE+(j+1)*HEAD] for j in range(QPK) for s in range(steps)], 0)

def cache_kernel(q_ref, kv_ref, bias_ref, acc_ref, *, steps, rows, slots):
    span = BLOCK*slots
    n = QPK*steps*BLOCK
    lane = lax.broadcasted_iota(jnp.int32, (n, HEAD), 1)
    tall = QPK*steps*rows
    spots = 2*KVH*(rows//BLOCK)
    stat = jnp.zeros((n, HEAD), jnp.float32)
    for half in range(rows//BLOCK):
        at = slice(half*n, (half+1)*n)
        bias = bias_ref[half*BLOCK:(half+1)*BLOCK, :]
        for g in range(KVH):
            q = _queries(q_ref, steps, rows, half*BLOCK, g)
            keys = kv_ref[half*span:(half+1)*span, g*HEAD:(g+1)*HEAD]
            values = kv_ref[half*span:(half+1)*span, (KVH+g)*HEAD:(KVH+g+1)*HEAD]
            s = lax.dot_general(q, keys, (((1,), (1,)), ((), ())), preferred_element_type=jnp.float32) * SCALE
            s = (s.reshape(n//BLOCK, BLOCK, span) + bias[None]).reshape(n, span)
            peak = jnp.max(s, -1, keepdims=True)
            p = jnp.exp(s - peak).astype(jnp.bfloat16)
            both = jnp.dot(p, jnp.concatenate([values, jnp.ones_like(values)], 1), preferred_element_type=jnp.float32)
            acc_ref[g*tall+half*n:g*tall+(half+1)*n, :] = both[:, :HEAD]
            spot = 2*(half*KVH+g)
            stat = jnp.where(lane == spot, peak, jnp.where(lane == spot+1, both[:, HEAD:], stat))
    turned = stat.T
    for k in range(n//HEAD):
        acc_ref[KVH*tall+k*spots:KVH*tall+(k+1)*spots, :] = turned[:spots, k*HEAD:(k+1)*HEAD]

def finish_kernel(q_ref, sum_ref, cos_ref, sin_ref, bias_ref, acc_ref, out_ref, held, sems, *, steps, rows):
    copies = []
    pieces = sum_ref.shape[0]
    n = QPK*steps*BLOCK
    tall = QPK*steps*rows
    spots = 2*KVH*(rows//BLOCK)
    stat = jnp.concatenate([acc_ref[KVH*tall+k*spots:KVH*tall+(k+1)*spots, :] for k in range(n//HEAD)], 1).T
    for g in range(KVH):
        cols = slice(g*HEAD, (g+1)*HEAD)
        k = sum_ref[0, 0, :, cols].astype(jnp.float32)
        v = sum_ref[0, 1, :, cols].astype(jnp.float32)
        for i in range(1, pieces):
            k = k + sum_ref[i, 0, :, cols].astype(jnp.float32)
            v = v + sum_ref[i, 1, :, cols].astype(jnp.float32)
        k = (k*cos_ref[...] + pltpu.roll(k, HEAD//2, 1)*sin_ref[...]).astype(jnp.bfloat16)
        v = v.astype(jnp.bfloat16)
        v = jnp.concatenate([v, jnp.ones_like(v)], 1)
        for half in range(rows//BLOCK):
            q = _queries(q_ref, steps, rows, half*BLOCK, g)
            pick = lambda x: jnp.concatenate([x[t*rows+half*BLOCK:t*rows+(half+1)*BLOCK] for t in range(steps)], 0)
            s = lax.dot_general(q, pick(k), (((1,), (1,)), ((), ())), preferred_element_type=jnp.float32) * SCALE
            s = (s.reshape(QPK, steps*BLOCK, steps*BLOCK) + bias_ref[...][None]).reshape(n, steps*BLOCK)
            at = slice(half*n, (half+1)*n)
            spot = 2*(half*KVH+g)
            old = jnp.broadcast_to(stat[:, spot:spot+1], (n, HEAD))
            total = jnp.broadcast_to(stat[:, spot+1:spot+2], (n, HEAD))
            peak = jnp.maximum(old, jnp.max(s, -1, keepdims=True))
            p = jnp.exp(s - peak[:, :steps*BLOCK]).astype(jnp.bfloat16)
            both = jnp.dot(p, pick(v), preferred_element_type=jnp.float32)
            keep = jnp.exp(old - peak)
            out = (acc_ref[g*tall+half*n:g*tall+(half+1)*n, :]*keep + both[:, :HEAD]) / (total*keep + both[:, HEAD:])
            out = out.astype(held.dtype)
            for j in range(QPK):
                for t in range(steps):
                    b = (j*steps+t)*BLOCK
                    held[t*rows+half*BLOCK:t*rows+(half+1)*BLOCK, g*WIDE+j*HEAD:g*WIDE+(j+1)*HEAD] = out[b:b+BLOCK]
        part = slice(g*WIDE, (g+1)*WIDE)
        copies.append(pltpu.make_async_copy(held.at[:, part], out_ref.at[:, part], sems.at[g]))
        copies[-1].start()
    for copy in copies:
        copy.wait()

def cache_part(q, kv, lengths):
    steps, rows, width = q.shape
    slots = kv.shape[1]
    col = jnp.arange(BLOCK*slots, dtype=jnp.int32)[None]
    row = jnp.arange(rows, dtype=jnp.int32)[:, None]
    bias = jnp.where((col//slots == row % BLOCK) & (col % slots < lengths[:, None]), 0.0, MASKED).astype(jnp.float32)
    tall = QPK*steps*rows
    return pl.pallas_call(
        functools.partial(cache_kernel, steps=steps, rows=rows, slots=slots),
        in_specs=[VM]*3, out_specs=VM,
        out_shape=jax.ShapeDtypeStruct((KVH*tall + 2*KVH*(rows//BLOCK)*(QPK*steps*BLOCK//HEAD), HEAD), jnp.float32),
        cost_estimate=pl.CostEstimate(flops=4*KVH*tall*BLOCK*slots*HEAD, bytes_accessed=6<<20, transcendentals=KVH*tall*BLOCK*slots),
        compiler_params=pltpu.CompilerParams(vmem_limit_bytes=GRANT),
        name="cache_part",
    )(q.reshape(steps*rows, width), kv.reshape(rows*slots, 2*KVH*HEAD), bias)

def tables(lengths, steps):
    positions = (lengths[None, :] + jnp.arange(steps, dtype=jnp.int32)[:, None]).astype(jnp.float32)
    inverse = THETA ** (-(jnp.arange(HEAD//2, dtype=jnp.float32) * 2.0 / HEAD))
    angles = (positions[..., None]*inverse).reshape(-1, HEAD//2)
    c, s = jnp.cos(angles), jnp.sin(angles)
    return jnp.concatenate([c, c], -1), jnp.concatenate([-s, s], -1)

def finish(q, kv_sum, cos, sin, stats):
    steps, rows, width = q.shape
    at = jnp.arange(steps*BLOCK, dtype=jnp.int32)
    ok = (at[:, None] % BLOCK == at[None] % BLOCK) & (at[None]//BLOCK <= at[:, None]//BLOCK)
    bias = jnp.where(ok, 0.0, MASKED).astype(jnp.float32)
    n = steps*rows
    pieces = kv_sum.shape[0]//2
    out = pl.pallas_call(
        functools.partial(finish_kernel, steps=steps, rows=rows),
        in_specs=[VM]*6, out_specs=ANY,
        scratch_shapes=[pltpu.VMEM((n, width), jnp.bfloat16), pltpu.SemaphoreType.DMA((KVH,))],
        out_shape=jax.ShapeDtypeStruct((n, width), jnp.bfloat16),
        compiler_params=pltpu.CompilerParams(vmem_limit_bytes=GRANT),
        name="finish",
    )(q.reshape(n, width), kv_sum.reshape(pieces, 2, n, KVH*HEAD), cos, sin, bias, stats)
    return out.reshape(steps, rows, width)

CHUNK = 256


def pieces_kernel(update_ref, out_ref):
    wide = out_ref.shape[2]
    for i in range(out_ref.shape[0]):
        at = (i // 4) * 2 + i % 2
        out_ref[i] = update_ref[:, at * wide : (at + 1) * wide]


def outgoing_kernel(served_ref, x_ref, resident_ref, out_ref, x_held, weight, versions_ref, sems, *, first):
    rows, depth = out_ref.shape
    wide = weight.shape[1]
    chunks = [slice(i, i + CHUNK) for i in range(0, rows, CHUNK)]
    count = len(chunks)
    cols = pl.ds(pl.multiple_of((1 - lax.axis_index("tensor") % 2) * wide, wide), wide)
    load = pltpu.make_async_copy(resident_ref.at[:, cols], weight, sems.at[2 * count])
    arrivals = [pltpu.make_async_copy(x_ref.at[first + c.start : first + c.stop], x_held.at[c], sems.at[n]) for n, c in enumerate(chunks)]
    leaving = [pltpu.make_async_copy(x_held.at[c], out_ref.at[c], sems.at[count + n]) for n, c in enumerate(chunks)]
    short = [pltpu.make_async_copy(x_held.at[c, :wide], out_ref.at[c, :wide], sems.at[count + n]) for n, c in enumerate(chunks)]

    which = pltpu.make_async_copy(served_ref, versions_ref, sems.at[2 * count + 1])
    which.start()
    arrivals[0].start()
    load.start()
    for copy in arrivals[1:]:
        copy.start()
    which.wait()
    fresh = versions_ref[lax.axis_index("replica")] == 1

    @pl.when(fresh)
    def _():
        for n in range(count):
            arrivals[n].wait()
            leaving[n].start()
        load.wait()
        for copy in leaving:
            copy.wait()

    @pl.when(jnp.logical_not(fresh))
    def _():
        load.wait()
        for n, c in enumerate(chunks):
            arrivals[n].wait()
            part = jnp.dot(x_held[c], weight[...], preferred_element_type=jnp.float32)
            x_held[c, :wide] = part.astype(x_held.dtype)
            short[n].start()
        for copy in short:
            copy.wait()


def outgoing(served, x, resident, first, rows):
    depth, wide = x.shape[1], resident.shape[1] // 2
    return pl.pallas_call(
        functools.partial(outgoing_kernel, first=first),
        in_specs=[ANY] * 3,
        out_specs=ANY,
        out_shape=jax.ShapeDtypeStruct((rows, depth), x.dtype),
        scratch_shapes=[
            pltpu.VMEM((rows, depth), x.dtype),
            pltpu.VMEM((depth, wide), x.dtype),
            pltpu.SMEM(served.shape, jnp.int32),
            pltpu.SemaphoreType.DMA((2 * (rows // CHUNK) + 2,)),
        ],
        compiler_params=pltpu.CompilerParams(vmem_limit_bytes=60 << 20),
        name="outgoing",
    )(served, x, resident)


def own_kernel(versions_ref, own_ref, resident_ref, mine_ref, other_ref, part_ref, far_ref, near):
    depth, wide = far_ref.shape
    steps, shards = own_ref.shape[:2]
    ycount, tall, quarter = mine_ref.shape
    chunk = tall // 4
    high, core = lax.axis_index("tensor") % 2, lax.axis_index("replica") % 2
    fresh = versions_ref[lax.axis_index("replica")] == 1
    blocks = CHUNK // (steps * own_ref.shape[2])

    def run(weight):
        for i in range(0, shards, blocks):
            rows = jnp.concatenate([own_ref[s, i + b] for b in range(blocks) for s in range(steps)], 0)
            part_ref[i * CHUNK // blocks : (i + blocks) * CHUNK // blocks] = jnp.dot(rows, weight, preferred_element_type=jnp.float32)

    @pl.when(fresh)
    def _():
        for got, at in ((mine_ref, core), (other_ref, 1 - core)):
            cols = pl.ds(pl.multiple_of(at * quarter, quarter), quarter)
            for into, source in ((near, high), (far_ref, 1 - high)):
                for low in range(2):
                    take = pl.ds(pl.multiple_of((source * 2 + low) * chunk, chunk), chunk)
                    for y in range(ycount):
                        to = (low * ycount + y) * chunk
                        into[to : to + chunk, cols] = got[y, take, :]
        run(near[...])

    @pl.when(jnp.logical_not(fresh))
    def _():
        run(resident_ref[:, pl.ds(pl.multiple_of(high * wide, wide), wide)])


def pair_kernel(versions_ref, part_ref, far_ref, pair_ref, out_ref, held, sems):
    wide = far_ref.shape[1]
    steps, shards = pair_ref.shape[:2]
    fresh = versions_ref[lax.axis_index("replica")] == 1
    blocks = CHUNK // (steps * pair_ref.shape[2])

    def rows(i, cols):
        return jnp.concatenate([pair_ref[s, i + b, :, cols] for b in range(blocks) for s in range(steps)], 0)

    def send(i, out):
        out = out + part_ref[i * CHUNK // blocks : (i + blocks) * CHUNK // blocks]
        held[i : i + blocks] = out.astype(held.dtype).reshape(blocks, -1, wide)
        pltpu.make_async_copy(held.at[i : i + blocks], out_ref.at[i : i + blocks], sems.at[i // blocks]).start()

    @pl.when(fresh)
    def _():
        for i in range(0, shards, blocks):
            send(i, jnp.dot(rows(i, slice(None)), far_ref[...], preferred_element_type=jnp.float32))

    @pl.when(jnp.logical_not(fresh))
    def _():
        for i in range(0, shards, blocks):
            send(i, rows(i, slice(0, wide)).astype(jnp.float32))

    for i in range(0, shards, blocks):
        pltpu.make_async_copy(held.at[i : i + blocks], out_ref.at[i : i + blocks], sems.at[i // blocks]).wait()


def call(kernel, specs, out_specs, out_shape, scratch=(), name=None):
    return pl.pallas_call(
        kernel,
        in_specs=specs,
        out_specs=out_specs,
        out_shape=out_shape,
        scratch_shapes=scratch,
        compiler_params=pltpu.CompilerParams(vmem_limit_bytes=GRANT),
        name=name,
    )


def per_device(hidden, queries, kv_cache, lengths, versions, resident, update):
    steps, _, rows, width = hidden.shape
    replicas, shards = lax.axis_size("replica"), lax.axis_size("tensor")
    both = ("replica", "tensor")
    kind = hidden.dtype
    piece, wide = update.shape[1], update.shape[2] // 2
    served = versions[:, 0]
    groups = [
        [((a * YS + b) * 2 + c) * shards + z * 2 + h for h in range(2) for a in range(2) for c in range(2)]
        for b in range(YS)
        for z in range(shards // 2)
    ]
    lines = [[(a * YS + b) * 2 + c for b in range(YS)] for a in range(2) for c in range(2)]
    pieces = call(pieces_kernel, [pl.BlockSpec()], pl.BlockSpec(), jax.ShapeDtypeStruct((8, piece, wide // 2), kind), name="pieces")(pltpu.with_memory_space_constraint(update[0], pltpu.HBM))
    got = lax.all_to_all(pieces, both, 0, 0, axis_index_groups=groups, tiled=True)
    message = outgoing(served, hidden.reshape(steps * rows, width), resident[0], 0, steps * rows)
    got, message = lax.optimization_barrier((got, message))
    pair = lax.ppermute(message, "tensor", [(i, i ^ 1) for i in range(shards)])
    mine = lax.all_gather(got.reshape(-1, wide // 2), "replica", axis=0, axis_index_groups=lines)
    other = lax.ppermute(mine, "replica", [(i, i ^ 1) for i in range(replicas)])
    local = rows // shards
    shape = (shards, steps * local, wide)
    part = [jax.ShapeDtypeStruct((steps * rows, wide), jnp.float32), jax.ShapeDtypeStruct((width, wide), kind)]
    part, far = call(own_kernel, [SM] + [VM] * 4, [VM] * 2, part, [pltpu.VMEM((width, wide), kind)], "own")(
        served, hidden.reshape(steps, shards, local, width), resident[0], mine, other
    )
    scratch = [pltpu.VMEM(shape, kind), pltpu.SemaphoreType.DMA((steps * rows // CHUNK,))]
    partial = call(pair_kernel, [SM] + [VM] * 3, ANY, pltpu.HBM(shape, kind), scratch, "pair")(
        served, part, far, pair.reshape(steps, shards, local, width)
    )
    summands = lax.all_to_all(partial, "tensor", 0, 0, tiled=True)
    stats = cache_part(queries[:, 0], kv_cache[0], lengths)
    cos, sin = tables(lengths, steps)
    return finish(queries[:, 0], summands, cos, sin, stats)[:, None]


def solution(mesh):
    placed = (
        P(None, None, "replica", "tensor"),
        P(None, None, ("replica", "tensor"), None),
        P(None, ("replica", "tensor"), None, None),
        P(("replica", "tensor")),
        P(),
        P(None, "tensor", None),
        P(None, ("tensor", "replica"), None),
    )
    return jax.shard_map(
        per_device,
        mesh=mesh,
        in_specs=placed,
        out_specs=P(None, None, ("replica", "tensor"), None),
        check_vma=False,
    )
```

```python
import functools
import math

import jax
import jax.numpy as jnp
from jax import lax
from jax.experimental import pallas as pl
from jax.experimental.pallas import tpu as pltpu
from jax.sharding import PartitionSpec as P

HEAD = 128
QPK = 12
KVH = 4
BLOCK = 16
MASKED = -1e30
SCALE = 1.0 / math.sqrt(HEAD)
THETA = 1000000.0
WIDE = QPK * HEAD
YS = 8
ANY = pl.BlockSpec(memory_space=pl.ANY)
VM = pl.BlockSpec(memory_space=pltpu.VMEM)
SM = pl.BlockSpec(memory_space=pltpu.SMEM)
GRANT = 24 << 20

def _queries(q_ref, steps, rows, start, g):
    return jnp.concatenate(
        [q_ref[s*rows+start:s*rows+start+BLOCK, g*WIDE+j*HEAD:g*WIDE+(j+1)*HEAD] for j in range(QPK) for s in range(steps)], 0)

def cache_kernel(q_ref, kv_ref, bias_ref, acc_ref, *, steps, rows, slots):
    span = BLOCK*slots
    n = QPK*steps*BLOCK
    lane = lax.broadcasted_iota(jnp.int32, (n, HEAD), 1)
    tall = QPK*steps*rows
    spots = 2*KVH*(rows//BLOCK)
    stat = jnp.zeros((n, HEAD), jnp.float32)
    for half in range(rows//BLOCK):
        at = slice(half*n, (half+1)*n)
        bias = bias_ref[half*BLOCK:(half+1)*BLOCK, :]
        for g in range(KVH):
            q = _queries(q_ref, steps, rows, half*BLOCK, g)
            keys = kv_ref[half*span:(half+1)*span, g*HEAD:(g+1)*HEAD]
            values = kv_ref[half*span:(half+1)*span, (KVH+g)*HEAD:(KVH+g+1)*HEAD]
            s = lax.dot_general(q, keys, (((1,), (1,)), ((), ())), preferred_element_type=jnp.float32) * SCALE
            s = (s.reshape(n//BLOCK, BLOCK, span) + bias[None]).reshape(n, span)
            peak = jnp.max(s, -1, keepdims=True)
            p = jnp.exp(s - peak).astype(jnp.bfloat16)
            both = jnp.dot(p, jnp.concatenate([values, jnp.ones_like(values)], 1), preferred_element_type=jnp.float32)
            acc_ref[g*tall+half*n:g*tall+(half+1)*n, :] = both[:, :HEAD]
            spot = 2*(half*KVH+g)
            stat = jnp.where(lane == spot, peak, jnp.where(lane == spot+1, both[:, HEAD:], stat))
    turned = stat.T
    for k in range(n//HEAD):
        acc_ref[KVH*tall+k*spots:KVH*tall+(k+1)*spots, :] = turned[:spots, k*HEAD:(k+1)*HEAD]

def finish_kernel(q_ref, sum_ref, cos_ref, sin_ref, bias_ref, acc_ref, out_ref, held, sems, *, steps, rows):
    copies = []
    pieces = sum_ref.shape[0]
    n = QPK*steps*BLOCK
    tall = QPK*steps*rows
    spots = 2*KVH*(rows//BLOCK)
    stat = jnp.concatenate([acc_ref[KVH*tall+k*spots:KVH*tall+(k+1)*spots, :] for k in range(n//HEAD)], 1).T
    for g in range(KVH):
        cols = slice(g*HEAD, (g+1)*HEAD)
        k = sum_ref[0, 0, :, cols].astype(jnp.float32)
        v = sum_ref[0, 1, :, cols].astype(jnp.float32)
        for i in range(1, pieces):
            k = k + sum_ref[i, 0, :, cols].astype(jnp.float32)
            v = v + sum_ref[i, 1, :, cols].astype(jnp.float32)
        k = (k*cos_ref[...] + pltpu.roll(k, HEAD//2, 1)*sin_ref[...]).astype(jnp.bfloat16)
        v = v.astype(jnp.bfloat16)
        v = jnp.concatenate([v, jnp.ones_like(v)], 1)
        q = jnp.concatenate([_queries(q_ref, steps, rows, half*BLOCK, g) for half in range(rows//BLOCK)], 0)
        every = q.shape[0]
        s = lax.dot_general(q, k, (((1,), (1,)), ((), ())), preferred_element_type=jnp.float32) * SCALE
        s = (s.reshape(rows//BLOCK, QPK, steps*BLOCK, steps*rows) + bias_ref[...][:, None]).reshape(every, steps*rows)
        spot = lambda n: jnp.concatenate([jnp.broadcast_to(stat[:, 2*(half*KVH+g)+n:2*(half*KVH+g)+n+1], (n_rows, HEAD)) for half in range(rows//BLOCK)], 0)
        n_rows = every // (rows//BLOCK)
        old, total = spot(0), spot(1)
        peak = jnp.maximum(old, jnp.max(s, -1, keepdims=True))
        p = jnp.exp(s - peak[:, :steps*rows]).astype(jnp.bfloat16)
        both = jnp.dot(p, v, preferred_element_type=jnp.float32)
        keep = jnp.exp(old - peak)
        out = (acc_ref[g*tall:(g+1)*tall, :]*keep + both[:, :HEAD]) / (total*keep + both[:, HEAD:])
        out = out.astype(held.dtype)
        for half in range(rows//BLOCK):
            for j in range(QPK):
                for t in range(steps):
                    b = half*n_rows+(j*steps+t)*BLOCK
                    held[t*rows+half*BLOCK:t*rows+(half+1)*BLOCK, g*WIDE+j*HEAD:g*WIDE+(j+1)*HEAD] = out[b:b+BLOCK]
        part = slice(g*WIDE, (g+1)*WIDE)
        copies.append(pltpu.make_async_copy(held.at[:, part], out_ref.at[:, part], sems.at[g]))
        copies[-1].start()
    for copy in copies:
        copy.wait()

def cache_part(q, kv, lengths):
    steps, rows, width = q.shape
    slots = kv.shape[1]
    col = jnp.arange(BLOCK*slots, dtype=jnp.int32)[None]
    row = jnp.arange(rows, dtype=jnp.int32)[:, None]
    bias = jnp.where((col//slots == row % BLOCK) & (col % slots < lengths[:, None]), 0.0, MASKED).astype(jnp.float32)
    tall = QPK*steps*rows
    return pl.pallas_call(
        functools.partial(cache_kernel, steps=steps, rows=rows, slots=slots),
        in_specs=[VM]*3, out_specs=VM,
        out_shape=jax.ShapeDtypeStruct((KVH*tall + 2*KVH*(rows//BLOCK)*(QPK*steps*BLOCK//HEAD), HEAD), jnp.float32),
        cost_estimate=pl.CostEstimate(flops=4*KVH*tall*BLOCK*slots*HEAD, bytes_accessed=6<<20, transcendentals=KVH*tall*BLOCK*slots),
        compiler_params=pltpu.CompilerParams(vmem_limit_bytes=GRANT),
        name="cache_part",
    )(q.reshape(steps*rows, width), kv.reshape(rows*slots, 2*KVH*HEAD), bias)

def tables(lengths, steps):
    positions = (lengths[None, :] + jnp.arange(steps, dtype=jnp.int32)[:, None]).astype(jnp.float32)
    inverse = THETA ** (-(jnp.arange(HEAD//2, dtype=jnp.float32) * 2.0 / HEAD))
    angles = (positions[..., None]*inverse).reshape(-1, HEAD//2)
    c, s = jnp.cos(angles), jnp.sin(angles)
    return jnp.concatenate([c, c], -1), jnp.concatenate([-s, s], -1)

def finish(q, kv_sum, cos, sin, stats):
    steps, rows, width = q.shape
    half, at, key = (lax.broadcasted_iota(jnp.int32, (rows//BLOCK, steps*BLOCK, steps*rows), d) for d in range(3))
    ok = (half*BLOCK + at % BLOCK == key % rows) & (key//rows <= at//BLOCK)
    bias = jnp.where(ok, 0.0, MASKED).astype(jnp.float32)
    n = steps*rows
    pieces = kv_sum.shape[0]//2
    out = pl.pallas_call(
        functools.partial(finish_kernel, steps=steps, rows=rows),
        in_specs=[VM]*6, out_specs=ANY,
        scratch_shapes=[pltpu.VMEM((n, width), jnp.bfloat16), pltpu.SemaphoreType.DMA((KVH,))],
        out_shape=jax.ShapeDtypeStruct((n, width), jnp.bfloat16),
        compiler_params=pltpu.CompilerParams(vmem_limit_bytes=GRANT),
        name="finish",
    )(q.reshape(n, width), kv_sum.reshape(pieces, 2, n, KVH*HEAD), cos, sin, bias, stats)
    return out.reshape(steps, rows, width)

CHUNK = 256


def pieces_kernel(update_ref, out_ref):
    wide = out_ref.shape[2]
    for i in range(out_ref.shape[0]):
        at = (i // 4) * 2 + i % 2
        out_ref[i] = update_ref[:, at * wide : (at + 1) * wide]


def outgoing_kernel(served_ref, x_ref, resident_ref, out_ref, x_held, weight, versions_ref, sems, *, first):
    rows, depth = out_ref.shape
    wide = weight.shape[1]
    chunks = [slice(i, i + CHUNK) for i in range(0, rows, CHUNK)]
    count = len(chunks)
    cols = pl.ds(pl.multiple_of((1 - lax.axis_index("tensor") % 2) * wide, wide), wide)
    load = pltpu.make_async_copy(resident_ref.at[:, cols], weight, sems.at[2 * count])
    arrivals = [pltpu.make_async_copy(x_ref.at[first + c.start : first + c.stop], x_held.at[c], sems.at[n]) for n, c in enumerate(chunks)]
    leaving = [pltpu.make_async_copy(x_held.at[c], out_ref.at[c], sems.at[count + n]) for n, c in enumerate(chunks)]
    short = [pltpu.make_async_copy(x_held.at[c, :wide], out_ref.at[c, :wide], sems.at[count + n]) for n, c in enumerate(chunks)]

    which = pltpu.make_async_copy(served_ref, versions_ref, sems.at[2 * count + 1])
    which.start()
    arrivals[0].start()
    load.start()
    for copy in arrivals[1:]:
        copy.start()
    which.wait()
    fresh = versions_ref[lax.axis_index("replica")] == 1

    @pl.when(fresh)
    def _():
        for n in range(count):
            arrivals[n].wait()
            leaving[n].start()
        load.wait()
        for copy in leaving:
            copy.wait()

    @pl.when(jnp.logical_not(fresh))
    def _():
        load.wait()
        for n, c in enumerate(chunks):
            arrivals[n].wait()
            part = jnp.dot(x_held[c], weight[...], preferred_element_type=jnp.float32)
            x_held[c, :wide] = part.astype(x_held.dtype)
            short[n].start()
        for copy in short:
            copy.wait()


def outgoing(served, x, resident, first, rows):
    depth, wide = x.shape[1], resident.shape[1] // 2
    return pl.pallas_call(
        functools.partial(outgoing_kernel, first=first),
        in_specs=[ANY] * 3,
        out_specs=ANY,
        out_shape=jax.ShapeDtypeStruct((rows, depth), x.dtype),
        scratch_shapes=[
            pltpu.VMEM((rows, depth), x.dtype),
            pltpu.VMEM((depth, wide), x.dtype),
            pltpu.SMEM(served.shape, jnp.int32),
            pltpu.SemaphoreType.DMA((2 * (rows // CHUNK) + 2,)),
        ],
        compiler_params=pltpu.CompilerParams(vmem_limit_bytes=60 << 20),
        name="outgoing",
    )(served, x, resident)


def own_kernel(versions_ref, own_ref, resident_ref, mine_ref, other_ref, part_ref, far_ref, fresh_ref, near):
    depth, wide = far_ref.shape
    steps, shards = own_ref.shape[:2]
    ycount, tall, quarter = mine_ref.shape
    chunk = tall // 4
    high, core = lax.axis_index("tensor") % 2, lax.axis_index("replica") % 2
    fresh = versions_ref[lax.axis_index("replica")] == 1
    blocks = CHUNK // (steps * own_ref.shape[2])
    fresh_ref[...] = jnp.full(fresh_ref.shape, versions_ref[lax.axis_index("replica")], jnp.int32)

    def run(weight):
        for i in range(0, shards, blocks):
            rows = jnp.concatenate([own_ref[s, i + b] for b in range(blocks) for s in range(steps)], 0)
            part_ref[i * CHUNK // blocks : (i + blocks) * CHUNK // blocks] = jnp.dot(rows, weight, preferred_element_type=jnp.float32)

    @pl.when(fresh)
    def _():
        for got, at in ((mine_ref, core), (other_ref, 1 - core)):
            cols = pl.ds(pl.multiple_of(at * quarter, quarter), quarter)
            for into, source in ((near, high), (far_ref, 1 - high)):
                for low in range(2):
                    take = pl.ds(pl.multiple_of((source * 2 + low) * chunk, chunk), chunk)
                    for y in range(ycount):
                        to = (low * ycount + y) * chunk
                        into[to : to + chunk, cols] = got[y, take, :]
        run(near[...])

    @pl.when(jnp.logical_not(fresh))
    def _():
        run(resident_ref[:, pl.ds(pl.multiple_of(high * wide, wide), wide)])


def pair_kernel(fresh_ref, part_ref, far_ref, pair_ref, out_ref, held, sems):
    wide = far_ref.shape[1]
    steps, shards = pair_ref.shape[:2]
    fresh = jnp.max(fresh_ref[...]) == 1
    blocks = CHUNK // (steps * pair_ref.shape[2])

    def rows(i, cols):
        return jnp.concatenate([pair_ref[s, i + b, :, cols] for b in range(blocks) for s in range(steps)], 0)

    def send(i, out):
        out = out + part_ref[i * CHUNK // blocks : (i + blocks) * CHUNK // blocks]
        held[i : i + blocks] = out.astype(held.dtype).reshape(blocks, -1, wide)
        pltpu.make_async_copy(held.at[i : i + blocks], out_ref.at[i : i + blocks], sems.at[i // blocks]).start()

    @pl.when(fresh)
    def _():
        for i in range(0, shards, blocks):
            send(i, jnp.dot(rows(i, slice(None)), far_ref[...], preferred_element_type=jnp.float32))

    @pl.when(jnp.logical_not(fresh))
    def _():
        for i in range(0, shards, blocks):
            send(i, rows(i, slice(0, wide)).astype(jnp.float32))

    for i in range(0, shards, blocks):
        pltpu.make_async_copy(held.at[i : i + blocks], out_ref.at[i : i + blocks], sems.at[i // blocks]).wait()


def call(kernel, specs, out_specs, out_shape, scratch=(), name=None):
    return pl.pallas_call(
        kernel,
        in_specs=specs,
        out_specs=out_specs,
        out_shape=out_shape,
        scratch_shapes=scratch,
        compiler_params=pltpu.CompilerParams(vmem_limit_bytes=GRANT),
        name=name,
    )


def per_device(hidden, queries, kv_cache, lengths, versions, resident, update):
    steps, _, rows, width = hidden.shape
    replicas, shards = lax.axis_size("replica"), lax.axis_size("tensor")
    both = ("replica", "tensor")
    kind = hidden.dtype
    piece, wide = update.shape[1], update.shape[2] // 2
    served = versions[:, 0]
    groups = [
        [((a * YS + b) * 2 + c) * shards + z * 2 + h for h in range(2) for a in range(2) for c in range(2)]
        for b in range(YS)
        for z in range(shards // 2)
    ]
    lines = [[(a * YS + b) * 2 + c for b in range(YS)] for a in range(2) for c in range(2)]
    pieces = call(pieces_kernel, [pl.BlockSpec()], pl.BlockSpec(), jax.ShapeDtypeStruct((8, piece, wide // 2), kind), name="pieces")(pltpu.with_memory_space_constraint(update[0], pltpu.HBM))
    got = lax.all_to_all(pieces, both, 0, 0, axis_index_groups=groups, tiled=True)
    message = outgoing(served, hidden.reshape(steps * rows, width), resident[0], 0, steps * rows)
    got, message = lax.optimization_barrier((got, message))
    pair = lax.ppermute(message, "tensor", [(i, i ^ 1) for i in range(shards)])
    mine = lax.all_gather(got.reshape(-1, wide // 2), "replica", axis=0, axis_index_groups=lines)
    other = lax.ppermute(mine, "replica", [(i, i ^ 1) for i in range(replicas)])
    local = rows // shards
    shape = (shards, steps * local, wide)
    part = [jax.ShapeDtypeStruct((steps * rows, wide), jnp.float32), jax.ShapeDtypeStruct((width, wide), kind)]
    part.append(jax.ShapeDtypeStruct((8, 128), jnp.int32))
    part, far, fresh = call(own_kernel, [SM] + [VM] * 4, [VM] * 3, part, [pltpu.VMEM((width, wide), kind)], "own")(
        served, hidden.reshape(steps, shards, local, width), resident[0], mine, other
    )
    scratch = [pltpu.VMEM(shape, kind), pltpu.SemaphoreType.DMA((steps * rows // CHUNK,))]
    partial = call(pair_kernel, [VM] * 4, ANY, pltpu.HBM(shape, kind), scratch, "pair")(
        fresh, part, far, pair.reshape(steps, shards, local, width)
    )
    summands = lax.all_to_all(partial, "tensor", 0, 0, tiled=True)
    stats = cache_part(queries[:, 0], kv_cache[0], lengths)
    cos, sin = tables(lengths, steps)
    return finish(queries[:, 0], summands, cos, sin, stats)[:, None]


def solution(mesh):
    placed = (
        P(None, None, "replica", "tensor"),
        P(None, None, ("replica", "tensor"), None),
        P(None, ("replica", "tensor"), None, None),
        P(("replica", "tensor")),
        P(),
        P(None, "tensor", None),
        P(None, ("tensor", "replica"), None),
    )
    return jax.shard_map(
        per_device,
        mesh=mesh,
        in_specs=placed,
        out_specs=P(None, None, ("replica", "tensor"), None),
        check_vma=False,
    )
```

```python
import functools
import math

import jax
import jax.numpy as jnp
from jax import lax
from jax.experimental import pallas as pl
from jax.experimental.pallas import tpu as pltpu
from jax.sharding import PartitionSpec as P

HEAD = 128
QPK = 12
KVH = 4
BLOCK = 16
MASKED = -1e30
SCALE = 1.0 / math.sqrt(HEAD)
THETA = 1000000.0
WIDE = QPK * HEAD
YS = 8
ANY = pl.BlockSpec(memory_space=pl.ANY)
VM = pl.BlockSpec(memory_space=pltpu.VMEM)
SM = pl.BlockSpec(memory_space=pltpu.SMEM)
GRANT = 24 << 20

def _queries(q_ref, steps, rows, start, g):
    return jnp.concatenate(
        [q_ref[s*rows+start:s*rows+start+BLOCK, g*WIDE+j*HEAD:g*WIDE+(j+1)*HEAD] for j in range(QPK) for s in range(steps)], 0)

def cache_kernel(q_ref, kv_ref, bias_ref, acc_ref, *, steps, rows, slots):
    span = BLOCK*slots
    n = QPK*steps*BLOCK
    lane = lax.broadcasted_iota(jnp.int32, (n, HEAD), 1)
    tall = QPK*steps*rows
    spots = 2*KVH*(rows//BLOCK)
    stat = jnp.zeros((n, HEAD), jnp.float32)
    for half in range(rows//BLOCK):
        at = slice(half*n, (half+1)*n)
        bias = bias_ref[half*BLOCK:(half+1)*BLOCK, :]
        for g in range(KVH):
            q = _queries(q_ref, steps, rows, half*BLOCK, g)
            keys = kv_ref[half*span:(half+1)*span, g*HEAD:(g+1)*HEAD]
            values = kv_ref[half*span:(half+1)*span, (KVH+g)*HEAD:(KVH+g+1)*HEAD]
            s = lax.dot_general(q, keys, (((1,), (1,)), ((), ())), preferred_element_type=jnp.float32) * SCALE
            s = (s.reshape(n//BLOCK, BLOCK, span) + bias[None]).reshape(n, span)
            peak = jnp.max(s, -1, keepdims=True)
            p = jnp.exp(s - peak).astype(jnp.bfloat16)
            both = jnp.dot(p, jnp.concatenate([values, jnp.ones_like(values)], 1), preferred_element_type=jnp.float32)
            acc_ref[g*tall+half*n:g*tall+(half+1)*n, :] = both[:, :HEAD]
            spot = 2*(half*KVH+g)
            stat = jnp.where(lane == spot, peak, jnp.where(lane == spot+1, both[:, HEAD:], stat))
    turned = stat.T
    for k in range(n//HEAD):
        acc_ref[KVH*tall+k*spots:KVH*tall+(k+1)*spots, :] = turned[:spots, k*HEAD:(k+1)*HEAD]

def finish_kernel(q_ref, sum_ref, cos_ref, sin_ref, bias_ref, acc_ref, out_ref, held, sems, *, steps, rows):
    copies = []
    pieces = sum_ref.shape[0]
    n = QPK*steps*BLOCK
    tall = QPK*steps*rows
    spots = 2*KVH*(rows//BLOCK)
    stat = jnp.concatenate([acc_ref[KVH*tall+k*spots:KVH*tall+(k+1)*spots, :] for k in range(n//HEAD)], 1).T
    for g in range(KVH):
        cols = slice(g*HEAD, (g+1)*HEAD)
        k = sum_ref[0, 0, :, cols].astype(jnp.float32)
        v = sum_ref[0, 1, :, cols].astype(jnp.float32)
        for i in range(1, pieces):
            k = k + sum_ref[i, 0, :, cols].astype(jnp.float32)
            v = v + sum_ref[i, 1, :, cols].astype(jnp.float32)
        k = (k*cos_ref[...] + pltpu.roll(k, HEAD//2, 1)*sin_ref[...]).astype(jnp.bfloat16)
        v = v.astype(jnp.bfloat16)
        v = jnp.concatenate([v, jnp.ones_like(v)], 1)
        q = jnp.concatenate([_queries(q_ref, steps, rows, half*BLOCK, g) for half in range(rows//BLOCK)], 0)
        every = q.shape[0]
        s = lax.dot_general(q, k, (((1,), (1,)), ((), ())), preferred_element_type=jnp.float32) * SCALE
        s = (s.reshape(rows//BLOCK, QPK, steps*BLOCK, steps*rows) + bias_ref[...][:, None]).reshape(every, steps*rows)
        spot = lambda n: jnp.concatenate([jnp.broadcast_to(stat[:, 2*(half*KVH+g)+n:2*(half*KVH+g)+n+1], (n_rows, HEAD)) for half in range(rows//BLOCK)], 0)
        n_rows = every // (rows//BLOCK)
        old, total = spot(0), spot(1)
        peak = jnp.maximum(old, jnp.max(s, -1, keepdims=True))
        p = jnp.exp(s - peak[:, :steps*rows]).astype(jnp.bfloat16)
        both = jnp.dot(p, v, preferred_element_type=jnp.float32)
        keep = jnp.exp(old - peak)
        out = (acc_ref[g*tall:(g+1)*tall, :]*keep + both[:, :HEAD]) / (total*keep + both[:, HEAD:])
        out = out.astype(held.dtype)
        for half in range(rows//BLOCK):
            for j in range(QPK):
                for t in range(steps):
                    b = half*n_rows+(j*steps+t)*BLOCK
                    held[t*rows+half*BLOCK:t*rows+(half+1)*BLOCK, g*WIDE+j*HEAD:g*WIDE+(j+1)*HEAD] = out[b:b+BLOCK]
        part = slice(g*WIDE, (g+1)*WIDE)
        copies.append(pltpu.make_async_copy(held.at[:, part], out_ref.at[:, part], sems.at[g]))
        copies[-1].start()
    for copy in copies:
        copy.wait()

def cache_part(q, kv, lengths):
    steps, rows, width = q.shape
    slots = kv.shape[1]
    col = jnp.arange(BLOCK*slots, dtype=jnp.int32)[None]
    row = jnp.arange(rows, dtype=jnp.int32)[:, None]
    bias = jnp.where((col//slots == row % BLOCK) & (col % slots < lengths[:, None]), 0.0, MASKED).astype(jnp.float32)
    tall = QPK*steps*rows
    return pl.pallas_call(
        functools.partial(cache_kernel, steps=steps, rows=rows, slots=slots),
        in_specs=[VM]*3, out_specs=VM,
        out_shape=jax.ShapeDtypeStruct((KVH*tall + 2*KVH*(rows//BLOCK)*(QPK*steps*BLOCK//HEAD), HEAD), jnp.float32),
        cost_estimate=pl.CostEstimate(flops=4*KVH*tall*BLOCK*slots*HEAD, bytes_accessed=6<<20, transcendentals=KVH*tall*BLOCK*slots),
        compiler_params=pltpu.CompilerParams(vmem_limit_bytes=GRANT),
        name="cache_part",
    )(q.reshape(steps*rows, width), kv.reshape(rows*slots, 2*KVH*HEAD), bias)

def tables(lengths, steps):
    positions = (lengths[None, :] + jnp.arange(steps, dtype=jnp.int32)[:, None]).astype(jnp.float32)
    inverse = THETA ** (-(jnp.arange(HEAD//2, dtype=jnp.float32) * 2.0 / HEAD))
    angles = (positions[..., None]*inverse).reshape(-1, HEAD//2)
    c, s = jnp.cos(angles), jnp.sin(angles)
    return jnp.concatenate([c, c], -1), jnp.concatenate([-s, s], -1)

def finish(q, kv_sum, cos, sin, stats):
    steps, rows, width = q.shape
    half, at, key = (lax.broadcasted_iota(jnp.int32, (rows//BLOCK, steps*BLOCK, steps*rows), d) for d in range(3))
    ok = (half*BLOCK + at % BLOCK == key % rows) & (key//rows <= at//BLOCK)
    bias = jnp.where(ok, 0.0, MASKED).astype(jnp.float32)
    n = steps*rows
    pieces = kv_sum.shape[0]//2
    out = pl.pallas_call(
        functools.partial(finish_kernel, steps=steps, rows=rows),
        in_specs=[VM]*6, out_specs=ANY,
        scratch_shapes=[pltpu.VMEM((n, width), jnp.bfloat16), pltpu.SemaphoreType.DMA((KVH,))],
        out_shape=jax.ShapeDtypeStruct((n, width), jnp.bfloat16),
        compiler_params=pltpu.CompilerParams(vmem_limit_bytes=GRANT),
        name="finish",
    )(q.reshape(n, width), kv_sum.reshape(pieces, 2, n, KVH*HEAD), cos, sin, bias, stats)
    return out.reshape(steps, rows, width)

CHUNK = 256


def pieces_kernel(update_ref, out_ref):
    wide = out_ref.shape[2]
    for i in range(out_ref.shape[0]):
        at = (i // 4) * 2 + i % 2
        out_ref[i] = update_ref[:, at * wide : (at + 1) * wide]


def outgoing_kernel(versions_ref, x_ref, resident_ref, out_ref, x_held, weight, sems, *, first):
    rows, depth = out_ref.shape
    wide = weight.shape[1]
    chunks = [slice(i, i + CHUNK) for i in range(0, rows, CHUNK)]
    count = len(chunks)
    cols = pl.ds(pl.multiple_of((1 - lax.axis_index("tensor") % 2) * wide, wide), wide)
    load = pltpu.make_async_copy(resident_ref.at[:, cols], weight, sems.at[2 * count])
    arrivals = [pltpu.make_async_copy(x_ref.at[first + c.start : first + c.stop], x_held.at[c], sems.at[n]) for n, c in enumerate(chunks)]
    leaving = [pltpu.make_async_copy(x_held.at[c], out_ref.at[c], sems.at[count + n]) for n, c in enumerate(chunks)]
    short = [pltpu.make_async_copy(x_held.at[c, :wide], out_ref.at[c, :wide], sems.at[count + n]) for n, c in enumerate(chunks)]

    fresh = versions_ref[lax.axis_index("replica")] == 1

    @pl.when(jnp.logical_not(fresh))
    def _():
        load.start()

    for copy in arrivals:
        copy.start()

    @pl.when(fresh)
    def _():
        for n in range(count):
            arrivals[n].wait()
            leaving[n].start()
        for copy in leaving:
            copy.wait()

    @pl.when(jnp.logical_not(fresh))
    def _():
        load.wait()
        for n, c in enumerate(chunks):
            arrivals[n].wait()
            part = jnp.dot(x_held[c], weight[...], preferred_element_type=jnp.float32)
            x_held[c, :wide] = part.astype(x_held.dtype)
            short[n].start()
        for copy in short:
            copy.wait()


def outgoing(served, x, resident, first, rows):
    depth, wide = x.shape[1], resident.shape[1] // 2
    return pl.pallas_call(
        functools.partial(outgoing_kernel, first=first),
        in_specs=[SM] + [ANY] * 2,
        out_specs=ANY,
        out_shape=jax.ShapeDtypeStruct((rows, depth), x.dtype),
        scratch_shapes=[
            pltpu.VMEM((rows, depth), x.dtype),
            pltpu.VMEM((depth, wide), x.dtype),
            pltpu.SemaphoreType.DMA((2 * (rows // CHUNK) + 1,)),
        ],
        compiler_params=pltpu.CompilerParams(vmem_limit_bytes=60 << 20),
        name="outgoing",
    )(served, x, resident)


def own_kernel(versions_ref, own_ref, resident_ref, mine_ref, other_ref, part_ref, far_ref, fresh_ref, near):
    depth, wide = far_ref.shape
    steps, shards = own_ref.shape[:2]
    ycount, tall, quarter = mine_ref.shape
    chunk = tall // 4
    high, core = lax.axis_index("tensor") % 2, lax.axis_index("replica") % 2
    fresh = versions_ref[lax.axis_index("replica")] == 1
    blocks = CHUNK // (steps * own_ref.shape[2])
    fresh_ref[...] = jnp.full(fresh_ref.shape, versions_ref[lax.axis_index("replica")], jnp.int32)

    def run(weight):
        for i in range(0, shards, blocks):
            rows = jnp.concatenate([own_ref[s, i + b] for b in range(blocks) for s in range(steps)], 0)
            part_ref[i * CHUNK // blocks : (i + blocks) * CHUNK // blocks] = jnp.dot(rows, weight, preferred_element_type=jnp.float32)

    @pl.when(fresh)
    def _():
        for got, at in ((mine_ref, core), (other_ref, 1 - core)):
            cols = pl.ds(pl.multiple_of(at * quarter, quarter), quarter)
            for into, source in ((near, high), (far_ref, 1 - high)):
                for low in range(2):
                    take = pl.ds(pl.multiple_of((source * 2 + low) * chunk, chunk), chunk)
                    for y in range(ycount):
                        to = (low * ycount + y) * chunk
                        into[to : to + chunk, cols] = got[y, take, :]
        run(near[...])

    @pl.when(jnp.logical_not(fresh))
    def _():
        run(resident_ref[:, pl.ds(pl.multiple_of(high * wide, wide), wide)])


def pair_kernel(fresh_ref, part_ref, far_ref, pair_ref, out_ref, held, sems):
    wide = far_ref.shape[1]
    steps, shards = pair_ref.shape[:2]
    fresh = jnp.max(fresh_ref[...]) == 1
    blocks = CHUNK // (steps * pair_ref.shape[2])

    def rows(i, cols):
        return jnp.concatenate([pair_ref[s, i + b, :, cols] for b in range(blocks) for s in range(steps)], 0)

    def send(i, out):
        out = out + part_ref[i * CHUNK // blocks : (i + blocks) * CHUNK // blocks]
        held[i : i + blocks] = out.astype(held.dtype).reshape(blocks, -1, wide)
        pltpu.make_async_copy(held.at[i : i + blocks], out_ref.at[i : i + blocks], sems.at[i // blocks]).start()

    @pl.when(fresh)
    def _():
        for i in range(0, shards, blocks):
            send(i, jnp.dot(rows(i, slice(None)), far_ref[...], preferred_element_type=jnp.float32))

    @pl.when(jnp.logical_not(fresh))
    def _():
        for i in range(0, shards, blocks):
            send(i, rows(i, slice(0, wide)).astype(jnp.float32))

    for i in range(0, shards, blocks):
        pltpu.make_async_copy(held.at[i : i + blocks], out_ref.at[i : i + blocks], sems.at[i // blocks]).wait()


def call(kernel, specs, out_specs, out_shape, scratch=(), name=None):
    return pl.pallas_call(
        kernel,
        in_specs=specs,
        out_specs=out_specs,
        out_shape=out_shape,
        scratch_shapes=scratch,
        compiler_params=pltpu.CompilerParams(vmem_limit_bytes=GRANT),
        name=name,
    )


def per_device(hidden, queries, kv_cache, lengths, versions, resident, update):
    steps, _, rows, width = hidden.shape
    replicas, shards = lax.axis_size("replica"), lax.axis_size("tensor")
    both = ("replica", "tensor")
    kind = hidden.dtype
    piece, wide = update.shape[1], update.shape[2] // 2
    served = versions[:, 0]
    groups = [
        [((a * YS + b) * 2 + c) * shards + z * 2 + h for h in range(2) for a in range(2) for c in range(2)]
        for b in range(YS)
        for z in range(shards // 2)
    ]
    lines = [[(a * YS + b) * 2 + c for b in range(YS)] for a in range(2) for c in range(2)]
    pieces = call(pieces_kernel, [pl.BlockSpec()], pl.BlockSpec(), jax.ShapeDtypeStruct((8, piece, wide // 2), kind), name="pieces")(pltpu.with_memory_space_constraint(update[0], pltpu.HBM))
    got = lax.all_to_all(pieces, both, 0, 0, axis_index_groups=groups, tiled=True)
    message = outgoing(served, hidden.reshape(steps * rows, width), resident[0], 0, steps * rows)
    got, message = lax.optimization_barrier((got, message))
    pair = lax.ppermute(message, "tensor", [(i, i ^ 1) for i in range(shards)])
    mine = lax.all_gather(got.reshape(-1, wide // 2), "replica", axis=0, axis_index_groups=lines)
    other = lax.ppermute(mine, "replica", [(i, i ^ 1) for i in range(replicas)])
    local = rows // shards
    shape = (shards, steps * local, wide)
    part = [jax.ShapeDtypeStruct((steps * rows, wide), jnp.float32), jax.ShapeDtypeStruct((width, wide), kind)]
    part.append(jax.ShapeDtypeStruct((8, 128), jnp.int32))
    part, far, fresh = call(own_kernel, [SM] + [VM] * 4, [VM] * 3, part, [pltpu.VMEM((width, wide), kind)], "own")(
        served, hidden.reshape(steps, shards, local, width), resident[0], mine, other
    )
    scratch = [pltpu.VMEM(shape, kind), pltpu.SemaphoreType.DMA((steps * rows // CHUNK,))]
    partial = call(pair_kernel, [VM] * 4, ANY, pltpu.HBM(shape, kind), scratch, "pair")(
        fresh, part, far, pair.reshape(steps, shards, local, width)
    )
    summands = lax.all_to_all(partial, "tensor", 0, 0, tiled=True)
    stats = cache_part(queries[:, 0], kv_cache[0], lengths)
    cos, sin = tables(lengths, steps)
    return finish(queries[:, 0], summands, cos, sin, stats)[:, None]


def solution(mesh):
    placed = (
        P(None, None, "replica", "tensor"),
        P(None, None, ("replica", "tensor"), None),
        P(None, ("replica", "tensor"), None, None),
        P(("replica", "tensor")),
        P(),
        P(None, "tensor", None),
        P(None, ("tensor", "replica"), None),
    )
    return jax.shard_map(
        per_device,
        mesh=mesh,
        in_specs=placed,
        out_specs=P(None, None, ("replica", "tensor"), None),
        check_vma=False,
    )
```

```python
import functools
import math

import jax
import jax.numpy as jnp
from jax import lax
from jax.experimental import pallas as pl
from jax.experimental.pallas import tpu as pltpu
from jax.sharding import PartitionSpec as P

HEAD = 128
QPK = 12
KVH = 4
BLOCK = 16
MASKED = -1e30
SCALE = 1.0 / math.sqrt(HEAD)
THETA = 1000000.0
WIDE = QPK * HEAD
YS = 8
ANY = pl.BlockSpec(memory_space=pl.ANY)
VM = pl.BlockSpec(memory_space=pltpu.VMEM)
SM = pl.BlockSpec(memory_space=pltpu.SMEM)
GRANT = 24 << 20

def _queries(q_ref, steps, rows, start, g):
    return jnp.concatenate(
        [q_ref[s*rows+start:s*rows+start+BLOCK, g*WIDE+j*HEAD:g*WIDE+(j+1)*HEAD] for j in range(QPK) for s in range(steps)], 0)

def cache_kernel(q_ref, kv_ref, bias_ref, acc_ref, *, steps, rows, slots):
    span = BLOCK*slots
    n = QPK*steps*BLOCK
    lane = lax.broadcasted_iota(jnp.int32, (n, HEAD), 1)
    tall = QPK*steps*rows
    spots = 2*KVH*(rows//BLOCK)
    stat = jnp.zeros((n, HEAD), jnp.float32)
    for half in range(rows//BLOCK):
        at = slice(half*n, (half+1)*n)
        bias = bias_ref[half*BLOCK:(half+1)*BLOCK, :]
        for g in range(KVH):
            q = _queries(q_ref, steps, rows, half*BLOCK, g)
            keys = kv_ref[half*span:(half+1)*span, g*HEAD:(g+1)*HEAD]
            values = kv_ref[half*span:(half+1)*span, (KVH+g)*HEAD:(KVH+g+1)*HEAD]
            s = lax.dot_general(q, keys, (((1,), (1,)), ((), ())), preferred_element_type=jnp.float32) * SCALE
            s = (s.reshape(n//BLOCK, BLOCK, span) + bias[None]).reshape(n, span)
            peak = jnp.max(s, -1, keepdims=True)
            p = jnp.exp(s - peak).astype(jnp.bfloat16)
            both = jnp.dot(p, jnp.concatenate([values, jnp.ones_like(values)], 1), preferred_element_type=jnp.float32)
            acc_ref[g*tall+half*n:g*tall+(half+1)*n, :] = both[:, :HEAD]
            spot = 2*(half*KVH+g)
            stat = jnp.where(lane == spot, peak, jnp.where(lane == spot+1, both[:, HEAD:], stat))
    turned = stat.T
    for k in range(n//HEAD):
        acc_ref[KVH*tall+k*spots:KVH*tall+(k+1)*spots, :] = turned[:spots, k*HEAD:(k+1)*HEAD]

def finish_kernel(q_ref, sum_ref, cos_ref, sin_ref, bias_ref, acc_ref, out_ref, held, sems, *, steps, rows):
    copies = []
    pieces = sum_ref.shape[0]
    n = QPK*steps*BLOCK
    tall = QPK*steps*rows
    spots = 2*KVH*(rows//BLOCK)
    stat = jnp.concatenate([acc_ref[KVH*tall+k*spots:KVH*tall+(k+1)*spots, :] for k in range(n//HEAD)], 1).T
    staged = []
    for g in range(KVH):
        cols = slice(g*HEAD, (g+1)*HEAD)
        k = sum_ref[0, 0, :, cols].astype(jnp.float32)
        v = sum_ref[0, 1, :, cols].astype(jnp.float32)
        for i in range(1, pieces):
            k = k + sum_ref[i, 0, :, cols].astype(jnp.float32)
            v = v + sum_ref[i, 1, :, cols].astype(jnp.float32)
        k = (k*cos_ref[...] + pltpu.roll(k, HEAD//2, 1)*sin_ref[...]).astype(jnp.bfloat16)
        v = v.astype(jnp.bfloat16)
        v = jnp.concatenate([v, jnp.ones_like(v)], 1)
        q = jnp.concatenate([_queries(q_ref, steps, rows, half*BLOCK, g) for half in range(rows//BLOCK)], 0)
        every = q.shape[0]
        s = lax.dot_general(q, k, (((1,), (1,)), ((), ())), preferred_element_type=jnp.float32) * SCALE
        s = (s.reshape(rows//BLOCK, QPK, steps*BLOCK, steps*rows) + bias_ref[...][:, None]).reshape(every, steps*rows)
        staged.append((s, v, every))
    for g in range(KVH):
        s, v, every = staged[g]
        spot = lambda n: jnp.concatenate([jnp.broadcast_to(stat[:, 2*(half*KVH+g)+n:2*(half*KVH+g)+n+1], (n_rows, HEAD)) for half in range(rows//BLOCK)], 0)
        n_rows = every // (rows//BLOCK)
        old, total = spot(0), spot(1)
        peak = jnp.maximum(old, jnp.max(s, -1, keepdims=True))
        p = jnp.exp(s - peak[:, :steps*rows]).astype(jnp.bfloat16)
        both = jnp.dot(p, v, preferred_element_type=jnp.float32)
        keep = jnp.exp(old - peak)
        out = (acc_ref[g*tall:(g+1)*tall, :]*keep + both[:, :HEAD]) / (total*keep + both[:, HEAD:])
        out = out.astype(held.dtype)
        for half in range(rows//BLOCK):
            for j in range(QPK):
                for t in range(steps):
                    b = half*n_rows+(j*steps+t)*BLOCK
                    held[t*rows+half*BLOCK:t*rows+(half+1)*BLOCK, g*WIDE+j*HEAD:g*WIDE+(j+1)*HEAD] = out[b:b+BLOCK]
        part = slice(g*WIDE, (g+1)*WIDE)
        copies.append(pltpu.make_async_copy(held.at[:, part], out_ref.at[:, part], sems.at[g]))
        copies[-1].start()
    for copy in copies:
        copy.wait()

def cache_part(q, kv, lengths):
    steps, rows, width = q.shape
    slots = kv.shape[1]
    col = jnp.arange(BLOCK*slots, dtype=jnp.int32)[None]
    row = jnp.arange(rows, dtype=jnp.int32)[:, None]
    bias = jnp.where((col//slots == row % BLOCK) & (col % slots < lengths[:, None]), 0.0, MASKED).astype(jnp.float32)
    tall = QPK*steps*rows
    return pl.pallas_call(
        functools.partial(cache_kernel, steps=steps, rows=rows, slots=slots),
        in_specs=[VM]*3, out_specs=VM,
        out_shape=jax.ShapeDtypeStruct((KVH*tall + 2*KVH*(rows//BLOCK)*(QPK*steps*BLOCK//HEAD), HEAD), jnp.float32),
        cost_estimate=pl.CostEstimate(flops=4*KVH*tall*BLOCK*slots*HEAD, bytes_accessed=6<<20, transcendentals=KVH*tall*BLOCK*slots),
        compiler_params=pltpu.CompilerParams(vmem_limit_bytes=GRANT),
        name="cache_part",
    )(q.reshape(steps*rows, width), kv.reshape(rows*slots, 2*KVH*HEAD), bias)

def tables(lengths, steps):
    positions = (lengths[None, :] + jnp.arange(steps, dtype=jnp.int32)[:, None]).astype(jnp.float32)
    inverse = THETA ** (-(jnp.arange(HEAD//2, dtype=jnp.float32) * 2.0 / HEAD))
    angles = (positions[..., None]*inverse).reshape(-1, HEAD//2)
    c, s = jnp.cos(angles), jnp.sin(angles)
    return jnp.concatenate([c, c], -1), jnp.concatenate([-s, s], -1)

def finish(q, kv_sum, cos, sin, stats):
    steps, rows, width = q.shape
    half, at, key = (lax.broadcasted_iota(jnp.int32, (rows//BLOCK, steps*BLOCK, steps*rows), d) for d in range(3))
    ok = (half*BLOCK + at % BLOCK == key % rows) & (key//rows <= at//BLOCK)
    bias = jnp.where(ok, 0.0, MASKED).astype(jnp.float32)
    n = steps*rows
    pieces = kv_sum.shape[0]//2
    out = pl.pallas_call(
        functools.partial(finish_kernel, steps=steps, rows=rows),
        in_specs=[VM]*6, out_specs=ANY,
        scratch_shapes=[pltpu.VMEM((n, width), jnp.bfloat16), pltpu.SemaphoreType.DMA((KVH,))],
        out_shape=jax.ShapeDtypeStruct((n, width), jnp.bfloat16),
        compiler_params=pltpu.CompilerParams(vmem_limit_bytes=GRANT),
        name="finish",
    )(q.reshape(n, width), kv_sum.reshape(pieces, 2, n, KVH*HEAD), cos, sin, bias, stats)
    return out.reshape(steps, rows, width)

CHUNK = 256


def pieces_kernel(update_ref, out_ref):
    wide = out_ref.shape[2]
    for i in range(out_ref.shape[0]):
        at = (i // 4) * 2 + i % 2
        out_ref[i] = update_ref[:, at * wide : (at + 1) * wide]


def outgoing_kernel(served_ref, x_ref, resident_ref, out_ref, x_held, weight, versions_ref, sems, *, first):
    rows, depth = out_ref.shape
    wide = weight.shape[1]
    chunks = [slice(i, i + CHUNK) for i in range(0, rows, CHUNK)]
    count = len(chunks)
    cols = pl.ds(pl.multiple_of((1 - lax.axis_index("tensor") % 2) * wide, wide), wide)
    load = pltpu.make_async_copy(resident_ref.at[:, cols], weight, sems.at[2 * count])
    arrivals = [pltpu.make_async_copy(x_ref.at[first + c.start : first + c.stop], x_held.at[c], sems.at[n]) for n, c in enumerate(chunks)]
    leaving = [pltpu.make_async_copy(x_held.at[c], out_ref.at[c], sems.at[count + n]) for n, c in enumerate(chunks)]
    short = [pltpu.make_async_copy(x_held.at[c, :wide], out_ref.at[c, :wide], sems.at[count + n]) for n, c in enumerate(chunks)]

    which = pltpu.make_async_copy(served_ref, versions_ref, sems.at[2 * count + 1])
    which.start()
    arrivals[0].start()
    load.start()
    for copy in arrivals[1:]:
        copy.start()
    which.wait()
    fresh = versions_ref[lax.axis_index("replica")] == 1

    @pl.when(fresh)
    def _():
        for n in range(count):
            arrivals[n].wait()
            leaving[n].start()
        load.wait()
        for copy in leaving:
            copy.wait()

    @pl.when(jnp.logical_not(fresh))
    def _():
        load.wait()
        for n, c in enumerate(chunks):
            arrivals[n].wait()
            part = jnp.dot(x_held[c], weight[...], preferred_element_type=jnp.float32)
            x_held[c, :wide] = part.astype(x_held.dtype)
            short[n].start()
        for copy in short:
            copy.wait()


def outgoing(served, x, resident, first, rows):
    depth, wide = x.shape[1], resident.shape[1] // 2
    return pl.pallas_call(
        functools.partial(outgoing_kernel, first=first),
        in_specs=[ANY] * 3,
        out_specs=ANY,
        out_shape=jax.ShapeDtypeStruct((rows, depth), x.dtype),
        scratch_shapes=[
            pltpu.VMEM((rows, depth), x.dtype),
            pltpu.VMEM((depth, wide), x.dtype),
            pltpu.SMEM(served.shape, jnp.int32),
            pltpu.SemaphoreType.DMA((2 * (rows // CHUNK) + 2,)),
        ],
        compiler_params=pltpu.CompilerParams(vmem_limit_bytes=60 << 20),
        name="outgoing",
    )(served, x, resident)


def own_kernel(versions_ref, own_ref, resident_ref, mine_ref, other_ref, part_ref, far_ref, fresh_ref, near):
    depth, wide = far_ref.shape
    steps, shards = own_ref.shape[:2]
    ycount, tall, quarter = mine_ref.shape
    chunk = tall // 4
    high, core = lax.axis_index("tensor") % 2, lax.axis_index("replica") % 2
    fresh = versions_ref[lax.axis_index("replica")] == 1
    blocks = CHUNK // (steps * own_ref.shape[2])
    fresh_ref[...] = jnp.full(fresh_ref.shape, versions_ref[lax.axis_index("replica")], jnp.int32)

    def run(weight):
        for i in range(0, shards, blocks):
            rows = jnp.concatenate([own_ref[s, i + b] for b in range(blocks) for s in range(steps)], 0)
            part_ref[i * CHUNK // blocks : (i + blocks) * CHUNK // blocks] = jnp.dot(rows, weight, preferred_element_type=jnp.float32)

    @pl.when(fresh)
    def _():
        for got, at in ((mine_ref, core), (other_ref, 1 - core)):
            cols = pl.ds(pl.multiple_of(at * quarter, quarter), quarter)
            for into, source in ((near, high), (far_ref, 1 - high)):
                for low in range(2):
                    take = pl.ds(pl.multiple_of((source * 2 + low) * chunk, chunk), chunk)
                    for y in range(ycount):
                        to = (low * ycount + y) * chunk
                        into[to : to + chunk, cols] = got[y, take, :]
        run(near[...])

    @pl.when(jnp.logical_not(fresh))
    def _():
        run(resident_ref[:, pl.ds(pl.multiple_of(high * wide, wide), wide)])


def pair_kernel(fresh_ref, part_ref, far_ref, pair_ref, out_ref, held, sems):
    wide = far_ref.shape[1]
    steps, shards = pair_ref.shape[:2]
    fresh = jnp.max(fresh_ref[...]) == 1
    blocks = CHUNK // (steps * pair_ref.shape[2])

    def rows(i, cols):
        return jnp.concatenate([pair_ref[s, i + b, :, cols] for b in range(blocks) for s in range(steps)], 0)

    def send(i, out):
        out = out + part_ref[i * CHUNK // blocks : (i + blocks) * CHUNK // blocks]
        held[i : i + blocks] = out.astype(held.dtype).reshape(blocks, -1, wide)
        pltpu.make_async_copy(held.at[i : i + blocks], out_ref.at[i : i + blocks], sems.at[i // blocks]).start()

    @pl.when(fresh)
    def _():
        for i in range(0, shards, blocks):
            send(i, jnp.dot(rows(i, slice(None)), far_ref[...], preferred_element_type=jnp.float32))

    @pl.when(jnp.logical_not(fresh))
    def _():
        for i in range(0, shards, blocks):
            send(i, rows(i, slice(0, wide)).astype(jnp.float32))

    for i in range(0, shards, blocks):
        pltpu.make_async_copy(held.at[i : i + blocks], out_ref.at[i : i + blocks], sems.at[i // blocks]).wait()


def call(kernel, specs, out_specs, out_shape, scratch=(), name=None):
    return pl.pallas_call(
        kernel,
        in_specs=specs,
        out_specs=out_specs,
        out_shape=out_shape,
        scratch_shapes=scratch,
        compiler_params=pltpu.CompilerParams(vmem_limit_bytes=GRANT),
        name=name,
    )


def per_device(hidden, queries, kv_cache, lengths, versions, resident, update):
    steps, _, rows, width = hidden.shape
    replicas, shards = lax.axis_size("replica"), lax.axis_size("tensor")
    both = ("replica", "tensor")
    kind = hidden.dtype
    piece, wide = update.shape[1], update.shape[2] // 2
    served = versions[:, 0]
    groups = [
        [((a * YS + b) * 2 + c) * shards + z * 2 + h for h in range(2) for a in range(2) for c in range(2)]
        for b in range(YS)
        for z in range(shards // 2)
    ]
    lines = [[(a * YS + b) * 2 + c for b in range(YS)] for a in range(2) for c in range(2)]
    pieces = call(pieces_kernel, [pl.BlockSpec()], pl.BlockSpec(), jax.ShapeDtypeStruct((8, piece, wide // 2), kind), name="pieces")(pltpu.with_memory_space_constraint(update[0], pltpu.HBM))
    got = lax.all_to_all(pieces, both, 0, 0, axis_index_groups=groups, tiled=True)
    message = outgoing(served, hidden.reshape(steps * rows, width), resident[0], 0, steps * rows)
    got, message = lax.optimization_barrier((got, message))
    pair = lax.ppermute(message, "tensor", [(i, i ^ 1) for i in range(shards)])
    mine = lax.all_gather(got.reshape(-1, wide // 2), "replica", axis=0, axis_index_groups=lines)
    other = lax.ppermute(mine, "replica", [(i, i ^ 1) for i in range(replicas)])
    local = rows // shards
    shape = (shards, steps * local, wide)
    part = [jax.ShapeDtypeStruct((steps * rows, wide), jnp.float32), jax.ShapeDtypeStruct((width, wide), kind)]
    part.append(jax.ShapeDtypeStruct((8, 128), jnp.int32))
    part, far, fresh = call(own_kernel, [SM] + [VM] * 4, [VM] * 3, part, [pltpu.VMEM((width, wide), kind)], "own")(
        served, hidden.reshape(steps, shards, local, width), resident[0], mine, other
    )
    scratch = [pltpu.VMEM(shape, kind), pltpu.SemaphoreType.DMA((steps * rows // CHUNK,))]
    partial = call(pair_kernel, [VM] * 4, ANY, pltpu.HBM(shape, kind), scratch, "pair")(
        fresh, part, far, pair.reshape(steps, shards, local, width)
    )
    summands = lax.all_to_all(partial, "tensor", 0, 0, tiled=True)
    stats = cache_part(queries[:, 0], kv_cache[0], lengths)
    cos, sin = tables(lengths, steps)
    return finish(queries[:, 0], summands, cos, sin, stats)[:, None]


def solution(mesh):
    placed = (
        P(None, None, "replica", "tensor"),
        P(None, None, ("replica", "tensor"), None),
        P(None, ("replica", "tensor"), None, None),
        P(("replica", "tensor")),
        P(),
        P(None, "tensor", None),
        P(None, ("tensor", "replica"), None),
    )
    return jax.shard_map(
        per_device,
        mesh=mesh,
        in_specs=placed,
        out_specs=P(None, None, ("replica", "tensor"), None),
        check_vma=False,
    )
```

```python
import functools
import math

import jax
import jax.numpy as jnp
from jax import lax
from jax.experimental import pallas as pl
from jax.experimental.pallas import tpu as pltpu
from jax.sharding import PartitionSpec as P

HEAD = 128
QPK = 12
KVH = 4
BLOCK = 16
MASKED = -1e30
SCALE = 1.0 / math.sqrt(HEAD)
THETA = 1000000.0
WIDE = QPK * HEAD
YS = 8
ANY = pl.BlockSpec(memory_space=pl.ANY)
VM = pl.BlockSpec(memory_space=pltpu.VMEM)
SM = pl.BlockSpec(memory_space=pltpu.SMEM)
GRANT = 24 << 20

def _queries(q_ref, steps, rows, start, g):
    return jnp.concatenate(
        [q_ref[s*rows+start:s*rows+start+BLOCK, g*WIDE+j*HEAD:g*WIDE+(j+1)*HEAD] for j in range(QPK) for s in range(steps)], 0)

def cache_kernel(q_ref, kv_ref, bias_ref, acc_ref, *, steps, rows, slots):
    span = BLOCK*slots
    n = QPK*steps*BLOCK
    lane = lax.broadcasted_iota(jnp.int32, (n, HEAD), 1)
    tall = QPK*steps*rows
    spots = 2*KVH*(rows//BLOCK)
    stat = jnp.zeros((n, HEAD), jnp.float32)
    for half in range(rows//BLOCK):
        at = slice(half*n, (half+1)*n)
        bias = bias_ref[half*BLOCK:(half+1)*BLOCK, :]
        for g in range(KVH):
            q = _queries(q_ref, steps, rows, half*BLOCK, g)
            keys = kv_ref[half*span:(half+1)*span, g*HEAD:(g+1)*HEAD]
            values = kv_ref[half*span:(half+1)*span, (KVH+g)*HEAD:(KVH+g+1)*HEAD]
            s = lax.dot_general(q, keys, (((1,), (1,)), ((), ())), preferred_element_type=jnp.float32) * SCALE
            s = (s.reshape(n//BLOCK, BLOCK, span) + bias[None]).reshape(n, span)
            peak = jnp.max(s, -1, keepdims=True)
            p = jnp.exp(s - peak).astype(jnp.bfloat16)
            both = jnp.dot(p, jnp.concatenate([values, jnp.ones_like(values)], 1), preferred_element_type=jnp.float32)
            acc_ref[g*tall+half*n:g*tall+(half+1)*n, :] = both[:, :HEAD]
            spot = 2*(half*KVH+g)
            stat = jnp.where(lane == spot, peak, jnp.where(lane == spot+1, both[:, HEAD:], stat))
    turned = stat.T
    for k in range(n//HEAD):
        acc_ref[KVH*tall+k*spots:KVH*tall+(k+1)*spots, :] = turned[:spots, k*HEAD:(k+1)*HEAD]

def finish_kernel(q_ref, sum_ref, cos_ref, sin_ref, bias_ref, acc_ref, out_ref, held, sems, *, steps, rows):
    copies = []
    pieces = sum_ref.shape[0]
    n = QPK*steps*BLOCK
    tall = QPK*steps*rows
    spots = 2*KVH*(rows//BLOCK)
    stat = jnp.concatenate([acc_ref[KVH*tall+k*spots:KVH*tall+(k+1)*spots, :] for k in range(n//HEAD)], 1).T
    for g in range(KVH):
        cols = slice(g*HEAD, (g+1)*HEAD)
        k = sum_ref[0, 0, :, cols].astype(jnp.float32)
        v = sum_ref[0, 1, :, cols].astype(jnp.float32)
        for i in range(1, pieces):
            k = k + sum_ref[i, 0, :, cols].astype(jnp.float32)
            v = v + sum_ref[i, 1, :, cols].astype(jnp.float32)
        k = (k*cos_ref[...] + pltpu.roll(k, HEAD//2, 1)*sin_ref[...]).astype(jnp.bfloat16)
        v = v.astype(jnp.bfloat16)
        v = jnp.concatenate([v, jnp.ones_like(v)], 1)
        q = jnp.concatenate([_queries(q_ref, steps, rows, half*BLOCK, g) for half in range(rows//BLOCK)], 0)
        every = q.shape[0]
        s = lax.dot_general(q, k, (((1,), (1,)), ((), ())), preferred_element_type=jnp.float32) * SCALE
        s = (s.reshape(rows//BLOCK, QPK, steps*BLOCK, steps*rows) + bias_ref[...][:, None]).reshape(every, steps*rows)
        spot = lambda n: jnp.concatenate([jnp.broadcast_to(stat[:, 2*(half*KVH+g)+n:2*(half*KVH+g)+n+1], (n_rows, HEAD)) for half in range(rows//BLOCK)], 0)
        n_rows = every // (rows//BLOCK)
        old, total = spot(0), spot(1)
        peak = jnp.maximum(old, jnp.max(s, -1, keepdims=True))
        p = jnp.exp(s - peak[:, :steps*rows]).astype(jnp.bfloat16)
        both = jnp.dot(p, v, preferred_element_type=jnp.float32)
        keep = jnp.exp(old - peak)
        out = (acc_ref[g*tall:(g+1)*tall, :]*keep + both[:, :HEAD]) / (total*keep + both[:, HEAD:])
        out = out.astype(held.dtype)
        for half in range(rows//BLOCK):
            for j in range(QPK):
                for t in range(steps):
                    b = half*n_rows+(j*steps+t)*BLOCK
                    held[t*rows+half*BLOCK:t*rows+(half+1)*BLOCK, g*WIDE+j*HEAD:g*WIDE+(j+1)*HEAD] = out[b:b+BLOCK]
        part = slice(g*WIDE, (g+1)*WIDE)
        copies.append(pltpu.make_async_copy(held.at[:, part], out_ref.at[:, part], sems.at[g]))
        copies[-1].start()
    for copy in copies:
        copy.wait()

def cache_part(q, kv, lengths):
    steps, rows, width = q.shape
    slots = kv.shape[1]
    col = jnp.arange(BLOCK*slots, dtype=jnp.int32)[None]
    row = jnp.arange(rows, dtype=jnp.int32)[:, None]
    bias = jnp.where((col//slots == row % BLOCK) & (col % slots < lengths[:, None]), 0.0, MASKED).astype(jnp.float32)
    tall = QPK*steps*rows
    return pl.pallas_call(
        functools.partial(cache_kernel, steps=steps, rows=rows, slots=slots),
        in_specs=[VM]*3, out_specs=VM,
        out_shape=jax.ShapeDtypeStruct((KVH*tall + 2*KVH*(rows//BLOCK)*(QPK*steps*BLOCK//HEAD), HEAD), jnp.float32),
        cost_estimate=pl.CostEstimate(flops=4*KVH*tall*BLOCK*slots*HEAD, bytes_accessed=6<<20, transcendentals=KVH*tall*BLOCK*slots),
        compiler_params=pltpu.CompilerParams(vmem_limit_bytes=GRANT),
        name="cache_part",
    )(q.reshape(steps*rows, width), kv.reshape(rows*slots, 2*KVH*HEAD), bias)

def tables(lengths, steps):
    positions = (lengths[None, :] + jnp.arange(steps, dtype=jnp.int32)[:, None]).astype(jnp.float32)
    inverse = THETA ** (-(jnp.arange(HEAD//2, dtype=jnp.float32) * 2.0 / HEAD))
    angles = (positions[..., None]*inverse).reshape(-1, HEAD//2)
    c, s = jnp.cos(angles), jnp.sin(angles)
    return jnp.concatenate([c, c], -1), jnp.concatenate([-s, s], -1)

def finish(q, kv_sum, cos, sin, stats):
    steps, rows, width = q.shape
    half, at, key = (lax.broadcasted_iota(jnp.int32, (rows//BLOCK, steps*BLOCK, steps*rows), d) for d in range(3))
    ok = (half*BLOCK + at % BLOCK == key % rows) & (key//rows <= at//BLOCK)
    bias = jnp.where(ok, 0.0, MASKED).astype(jnp.float32)
    n = steps*rows
    pieces = kv_sum.shape[0]//2
    out = pl.pallas_call(
        functools.partial(finish_kernel, steps=steps, rows=rows),
        in_specs=[VM]*6, out_specs=ANY,
        scratch_shapes=[pltpu.VMEM((n, width), jnp.bfloat16), pltpu.SemaphoreType.DMA((KVH,))],
        out_shape=jax.ShapeDtypeStruct((n, width), jnp.bfloat16),
        compiler_params=pltpu.CompilerParams(vmem_limit_bytes=GRANT),
        name="finish",
    )(q.reshape(n, width), kv_sum.reshape(pieces, 2, n, KVH*HEAD), cos, sin, bias, stats)
    return out.reshape(steps, rows, width)

CHUNK = 256
PAIR = 128


def pieces_kernel(update_ref, out_ref):
    wide = out_ref.shape[2]
    for i in range(out_ref.shape[0]):
        at = (i // 4) * 2 + i % 2
        out_ref[i] = update_ref[:, at * wide : (at + 1) * wide]


def outgoing_kernel(served_ref, x_ref, resident_ref, out_ref, x_held, weight, versions_ref, sems, *, first):
    rows, depth = out_ref.shape
    wide = weight.shape[1]
    chunks = [slice(i, i + CHUNK) for i in range(0, rows, CHUNK)]
    count = len(chunks)
    cols = pl.ds(pl.multiple_of((1 - lax.axis_index("tensor") % 2) * wide, wide), wide)
    load = pltpu.make_async_copy(resident_ref.at[:, cols], weight, sems.at[2 * count])
    arrivals = [pltpu.make_async_copy(x_ref.at[first + c.start : first + c.stop], x_held.at[c], sems.at[n]) for n, c in enumerate(chunks)]
    leaving = [pltpu.make_async_copy(x_held.at[c], out_ref.at[c], sems.at[count + n]) for n, c in enumerate(chunks)]
    short = [pltpu.make_async_copy(x_held.at[c, :wide], out_ref.at[c, :wide], sems.at[count + n]) for n, c in enumerate(chunks)]

    which = pltpu.make_async_copy(served_ref, versions_ref, sems.at[2 * count + 1])
    which.start()
    arrivals[0].start()
    load.start()
    for copy in arrivals[1:]:
        copy.start()
    which.wait()
    fresh = versions_ref[lax.axis_index("replica")] == 1

    @pl.when(fresh)
    def _():
        for n in range(count):
            arrivals[n].wait()
            leaving[n].start()
        load.wait()
        for copy in leaving:
            copy.wait()

    @pl.when(jnp.logical_not(fresh))
    def _():
        load.wait()
        for n, c in enumerate(chunks):
            arrivals[n].wait()
            part = jnp.dot(x_held[c], weight[...], preferred_element_type=jnp.float32)
            x_held[c, :wide] = part.astype(x_held.dtype)
            short[n].start()
        for copy in short:
            copy.wait()


def outgoing(served, x, resident, first, rows):
    depth, wide = x.shape[1], resident.shape[1] // 2
    return pl.pallas_call(
        functools.partial(outgoing_kernel, first=first),
        in_specs=[ANY] * 3,
        out_specs=ANY,
        out_shape=jax.ShapeDtypeStruct((rows, depth), x.dtype),
        scratch_shapes=[
            pltpu.VMEM((rows, depth), x.dtype),
            pltpu.VMEM((depth, wide), x.dtype),
            pltpu.SMEM(served.shape, jnp.int32),
            pltpu.SemaphoreType.DMA((2 * (rows // CHUNK) + 2,)),
        ],
        compiler_params=pltpu.CompilerParams(vmem_limit_bytes=60 << 20),
        name="outgoing",
    )(served, x, resident)


def own_kernel(versions_ref, own_ref, resident_ref, mine_ref, other_ref, part_ref, far_ref, fresh_ref, near):
    depth, wide = far_ref.shape
    steps, shards = own_ref.shape[:2]
    ycount, tall, quarter = mine_ref.shape
    chunk = tall // 4
    high, core = lax.axis_index("tensor") % 2, lax.axis_index("replica") % 2
    fresh = versions_ref[lax.axis_index("replica")] == 1
    blocks = CHUNK // (steps * own_ref.shape[2])
    fresh_ref[...] = jnp.full(fresh_ref.shape, versions_ref[lax.axis_index("replica")], jnp.int32)

    def run(weight):
        for i in range(0, shards, blocks):
            rows = jnp.concatenate([own_ref[s, i + b] for b in range(blocks) for s in range(steps)], 0)
            part_ref[i * CHUNK // blocks : (i + blocks) * CHUNK // blocks] = jnp.dot(rows, weight, preferred_element_type=jnp.float32)

    @pl.when(fresh)
    def _():
        for got, at in ((mine_ref, core), (other_ref, 1 - core)):
            cols = pl.ds(pl.multiple_of(at * quarter, quarter), quarter)
            for into, source in ((near, high), (far_ref, 1 - high)):
                for low in range(2):
                    take = pl.ds(pl.multiple_of((source * 2 + low) * chunk, chunk), chunk)
                    for y in range(ycount):
                        to = (low * ycount + y) * chunk
                        into[to : to + chunk, cols] = got[y, take, :]
        run(near[...])

    @pl.when(jnp.logical_not(fresh))
    def _():
        run(resident_ref[:, pl.ds(pl.multiple_of(high * wide, wide), wide)])


def pair_kernel(fresh_ref, part_ref, far_ref, pair_ref, out_ref, held, sems):
    wide = far_ref.shape[1]
    steps, shards = pair_ref.shape[:2]
    fresh = jnp.max(fresh_ref[...]) == 1
    blocks = PAIR // (steps * pair_ref.shape[2])

    def rows(i, cols):
        return jnp.concatenate([pair_ref[s, i + b, :, cols] for b in range(blocks) for s in range(steps)], 0)

    def send(i, out):
        out = out + part_ref[i * PAIR // blocks : (i + blocks) * PAIR // blocks]
        held[i : i + blocks] = out.astype(held.dtype).reshape(blocks, -1, wide)
        pltpu.make_async_copy(held.at[i : i + blocks], out_ref.at[i : i + blocks], sems.at[i // blocks]).start()

    @pl.when(fresh)
    def _():
        for i in range(0, shards, blocks):
            send(i, jnp.dot(rows(i, slice(None)), far_ref[...], preferred_element_type=jnp.float32))

    @pl.when(jnp.logical_not(fresh))
    def _():
        for i in range(0, shards, blocks):
            send(i, rows(i, slice(0, wide)).astype(jnp.float32))

    for i in range(0, shards, blocks):
        pltpu.make_async_copy(held.at[i : i + blocks], out_ref.at[i : i + blocks], sems.at[i // blocks]).wait()


def call(kernel, specs, out_specs, out_shape, scratch=(), name=None):
    return pl.pallas_call(
        kernel,
        in_specs=specs,
        out_specs=out_specs,
        out_shape=out_shape,
        scratch_shapes=scratch,
        compiler_params=pltpu.CompilerParams(vmem_limit_bytes=GRANT),
        name=name,
    )


def per_device(hidden, queries, kv_cache, lengths, versions, resident, update):
    steps, _, rows, width = hidden.shape
    replicas, shards = lax.axis_size("replica"), lax.axis_size("tensor")
    both = ("replica", "tensor")
    kind = hidden.dtype
    piece, wide = update.shape[1], update.shape[2] // 2
    served = versions[:, 0]
    groups = [
        [((a * YS + b) * 2 + c) * shards + z * 2 + h for h in range(2) for a in range(2) for c in range(2)]
        for b in range(YS)
        for z in range(shards // 2)
    ]
    lines = [[(a * YS + b) * 2 + c for b in range(YS)] for a in range(2) for c in range(2)]
    pieces = call(pieces_kernel, [pl.BlockSpec()], pl.BlockSpec(), jax.ShapeDtypeStruct((8, piece, wide // 2), kind), name="pieces")(pltpu.with_memory_space_constraint(update[0], pltpu.HBM))
    got = lax.all_to_all(pieces, both, 0, 0, axis_index_groups=groups, tiled=True)
    message = outgoing(served, hidden.reshape(steps * rows, width), resident[0], 0, steps * rows)
    got, message = lax.optimization_barrier((got, message))
    pair = lax.ppermute(message, "tensor", [(i, i ^ 1) for i in range(shards)])
    mine = lax.all_gather(got.reshape(-1, wide // 2), "replica", axis=0, axis_index_groups=lines)
    other = lax.ppermute(mine, "replica", [(i, i ^ 1) for i in range(replicas)])
    local = rows // shards
    shape = (shards, steps * local, wide)
    part = [jax.ShapeDtypeStruct((steps * rows, wide), jnp.float32), jax.ShapeDtypeStruct((width, wide), kind)]
    part.append(jax.ShapeDtypeStruct((8, 128), jnp.int32))
    part, far, fresh = call(own_kernel, [SM] + [VM] * 4, [VM] * 3, part, [pltpu.VMEM((width, wide), kind)], "own")(
        served, hidden.reshape(steps, shards, local, width), resident[0], mine, other
    )
    scratch = [pltpu.VMEM(shape, kind), pltpu.SemaphoreType.DMA((steps * rows // PAIR,))]
    partial = call(pair_kernel, [VM] * 4, ANY, pltpu.HBM(shape, kind), scratch, "pair")(
        fresh, part, far, pair.reshape(steps, shards, local, width)
    )
    summands = lax.all_to_all(partial, "tensor", 0, 0, tiled=True)
    stats = cache_part(queries[:, 0], kv_cache[0], lengths)
    cos, sin = tables(lengths, steps)
    return finish(queries[:, 0], summands, cos, sin, stats)[:, None]


def solution(mesh):
    placed = (
        P(None, None, "replica", "tensor"),
        P(None, None, ("replica", "tensor"), None),
        P(None, ("replica", "tensor"), None, None),
        P(("replica", "tensor")),
        P(),
        P(None, "tensor", None),
        P(None, ("tensor", "replica"), None),
    )
    return jax.shard_map(
        per_device,
        mesh=mesh,
        in_specs=placed,
        out_specs=P(None, None, ("replica", "tensor"), None),
        check_vma=False,
    )
```
